128 devices in a mesh: dp: 4 (over z_hi, core), dap: 32 (over y, z_lo, x).
Axes of the slice: x: 4, y: 4, z: 4 (z_hi: 2, z_lo: 2; z = z_hi * 2 + z_lo), core: 2. Of those that a mesh axis runs over, the one named last changes fastest.
Arguments:
- pair_in: bfloat16 [4, 256, 256, 128], P('dp', 'dap'), may hold values from -6 to 6
- residue_mask: int32 [4, 256], P('dp'), may hold values 0 or 1
- chain_index: int32 [4, 256], P('dp'), may hold values from 0 to 3, never falling along the last dimension, each value on 1 to 128 neighbouring positions
- chain_bias: float32 [128], replicated, may hold values from -3 to 3
- proj_weight: bfloat16 [2, 128, 640], replicated, may hold values from -0.5 to 0.5
- out_weight: bfloat16 [2, 128, 128], replicated, may hold values from -0.5 to 0.5
- cotangent: bfloat16 [4, 256, 256, 128], P('dp', 'dap'), may hold values from -6 to 6
Outputs:
- out_pair: bfloat16 [4, 256, 256, 128], P('dp', 'dap')
- pair_grad: bfloat16 [4, 256, 256, 128], P('dp', 'dap')
- grad_proj: float32 [2, 128, 640], replicated
- grad_out: float32 [2, 128, 128], replicated
- grad_chain: float32 [128], replicated
The draws below stay inside these ranges and needn't reach their ends.
Inputs may be any that keep to these rules, and one draw needn't show every extreme that they name: `residue_mask`: 1 marks a residue that takes part, 0 one that is masked out. `chain_index`: chain numbers never fall along a complex; each chain holds 1 to 128 residues.
All inputs are finite; a program needn't handle non-finite values. No bound on the sum of `residue_mask` on one device may be relied on, other than what follows from the above.
Results may differ from the reference program's by a relative error of at most 0.028.
Values may be sent and summed in bfloat16 or wider, within the bound.
A program may use at most 128 MiB of HBM per device.

```python
import math
import jax
import jax.numpy as jnp
import numpy as np
from jax import lax

C = 128
CHAINS = 4
NRES = 256
MEMBERS = 4


def touch_ends(array, rng, low, largest):
    dims = array.shape
    index_at = [jax.random.randint(jax.random.fold_in(rng, axis), (), 0, dims[axis]) for axis in range(len(dims))]
    array = array.at[tuple(index_at)].set(low)
    longest = dims.index(max(dims))
    index_at[longest] = (index_at[longest] + 1) % dims[longest]
    return array.at[tuple(index_at)].set(largest)


def levels(rng, shape, split, smallest, top_value):
    gain, own = 1.0, jax.random.fold_in(rng, 6)
    for dim, shards_of in split:
        draws = jnp.exp(jax.random.uniform(jax.random.fold_in(own, dim), (shards_of,), jnp.float32, smallest / len(split), top_value / len(split)))
        gain = gain * jnp.repeat(draws, shape[dim] // shards_of).reshape([-1 if axis == dim else 1 for axis in range(len(shape))])
    return gain


def length_profile(count, total, most, slope):
    weights = [(1 << 20) // math.isqrt(standing ** slope) + 1 for standing in range(2, count + 1)]
    spare, given = total - most - (count - 1), [1] * (count - 1)
    while spare > 0:
        candidates = [i for i in range(count - 1) if given[i] < most]
        whole, budget = sum([weights[i] for i in candidates]), spare
        for i in candidates:
            addition = min(most - given[i], max(1, budget * weights[i] // whole), spare)
            given[i] = given[i] + addition
            spare = spare - addition
    return np.array([most] + given)


def ragged(key, amount, total, most, lean):
    if amount == 2:
        one = jax.random.randint(key, (), max(1, total - most), min(most, total - 1) + 1)
        return jnp.stack([one, total - one])
    sizes = jnp.asarray(length_profile(amount, total, most, lean), jnp.int32)
    pairs = (amount - 1) // 2
    giver, receiver = sizes[1:1 + 2 * pairs:2], sizes[2:2 + 2 * pairs:2]
    margin = jnp.minimum(giver - 1, most - receiver)
    moved = jax.random.randint(jax.random.fold_in(key, 1), (pairs,), 0, 1 << 20) % (margin + 1)
    sizes = sizes.at[1:1 + 2 * pairs:2].set(giver - moved).at[2:2 + 2 * pairs:2].set(receiver + moved)
    return sizes[jax.random.permutation(jax.random.fold_in(key, 2), amount)]


def normal_values(key, shape, deviation, bound, cuts=(), held_as=jnp.bfloat16):
    values = deviation * jax.random.normal(key, shape, jnp.float32)
    if cuts:
        values = values * levels(key, shape, cuts, -0.22, 0.18)
    return jnp.clip(values, -bound, bound).astype(held_as)


def setup_inputs(seed: int = 0) -> dict:
    key_list = jax.random.split(jax.random.key(seed), 8)
    pair_in = normal_values(key_list[0], (MEMBERS, NRES, NRES, C), 1.0, 6.0, ((0, 4), (1, 32)))
    residue_mask = touch_ends((jax.random.randint(key_list[1], (MEMBERS, NRES), 0, 8) < 7).astype(jnp.int32), jax.random.fold_in(key_list[1], 1), 0, 1)
    chain_index = jax.vmap(lambda own: jnp.searchsorted(jnp.cumsum(ragged(own, CHAINS, NRES, NRES // 2, 1)), jnp.arange(NRES), side="right"))(jax.random.split(key_list[2], MEMBERS)).reshape((MEMBERS, NRES)).astype(jnp.int32)
    chain_bias = normal_values(key_list[3], (C,), 0.5, 3.0, (), jnp.float32)
    proj_weight = normal_values(key_list[4], (2, C, 5 * C), C ** -0.5, 0.5)
    out_weight = normal_values(key_list[5], (2, C, C), C ** -0.5, 0.5)
    cotangent = normal_values(key_list[6], (MEMBERS, NRES, NRES, C), 1.0, 6.0, ((0, 4), (1, 32)))
    return {"pair_in": pair_in, "residue_mask": residue_mask, "chain_index": chain_index, "chain_bias": chain_bias, "proj_weight": proj_weight, "out_weight": out_weight, "cotangent": cotangent}


EPSILON = 1e-05

def layer_norm(tensor):
    average = lax.optimization_barrier(jnp.mean(tensor, axis=-1, keepdims=True))
    centred = tensor - average
    variance = lax.optimization_barrier(jnp.mean(centred * centred, axis=-1, keepdims=True))
    inv_std = lax.rsqrt(variance + EPSILON)
    return (centred * inv_std, inv_std)

def norm_back(normed, inv_std, upstream):
    first_mean = lax.optimization_barrier(jnp.mean(upstream, axis=-1, keepdims=True))
    second_mean = lax.optimization_barrier(jnp.mean(upstream * normed, axis=-1, keepdims=True))
    return (upstream - first_mean - normed * second_mean) * inv_std

def front_values(pair_block, mask_rows, mask_cols, proj_w):
    row_count, column_count, channel_count = pair_block.shape
    normed, inv_std = layer_norm(pair_block.astype(jnp.float32))
    normed_b = normed.astype(jnp.bfloat16)
    projected = jnp.dot(normed_b.reshape(-1, channel_count), proj_w, preferred_element_type=jnp.float32)
    projected = projected.reshape(row_count, column_count, 5, channel_count)
    pair_mask = (mask_rows[:, None] * mask_cols[None, :])[:, :, None]
    left_edge = pair_mask * jax.nn.sigmoid(projected[:, :, 1]) * projected[:, :, 0]
    right_edge = pair_mask * jax.nn.sigmoid(projected[:, :, 3]) * projected[:, :, 2]
    gating = jax.nn.sigmoid(projected[:, :, 4])
    return (normed, inv_std, normed_b, projected, pair_mask, left_edge, right_edge, gating)

def rear_values(pair_block, product, gating, out_w):
    channel_count = product.shape[2]
    prod_normed, prod_inv = layer_norm(product.astype(jnp.float32))
    prod_normed_b = prod_normed.astype(jnp.bfloat16)
    update = jnp.dot(prod_normed_b.reshape(-1, channel_count), out_w, preferred_element_type=jnp.float32)
    update = update.reshape(product.shape)
    new_pair = (pair_block.astype(jnp.float32) + gating * update).astype(jnp.bfloat16)
    return (prod_normed, prod_inv, prod_normed_b, update, new_pair)

def rear_back(upstream, gating, out_w, rear):
    channel_count = upstream.shape[2]
    flowing = upstream.astype(jnp.float32)
    grad_gate = flowing * rear[3]
    grad_update = (flowing * gating).astype(jnp.bfloat16)
    flattened = grad_update.reshape(-1, channel_count)
    grad_out_w = jnp.dot(rear[2].reshape(-1, channel_count).T, flattened, preferred_element_type=jnp.float32)
    grad_normed = jnp.dot(flattened, out_w.T, preferred_element_type=jnp.float32).reshape(upstream.shape)
    grad_product = norm_back(rear[0], rear[1], grad_normed).astype(jnp.bfloat16)
    return (grad_gate, grad_product, grad_out_w)

def front_back(upstream, grad_left, grad_right, grad_gate, front, proj_w):
    channel_count = upstream.shape[2]
    projected = front[3]
    gating = front[7]
    left_sig = jax.nn.sigmoid(projected[:, :, 1])
    right_sig = jax.nn.sigmoid(projected[:, :, 3])
    masked_left = grad_left.astype(jnp.float32) * front[4]
    masked_right = grad_right.astype(jnp.float32) * front[4]
    blocks = [masked_left * left_sig, masked_left * projected[:, :, 0] * left_sig * (1.0 - left_sig), masked_right * right_sig, masked_right * projected[:, :, 2] * right_sig * (1.0 - right_sig), grad_gate * gating * (1.0 - gating)]
    grad_proj_b = jnp.stack(blocks, axis=2).reshape(-1, 5 * channel_count).astype(jnp.bfloat16)
    grad_proj_w = jnp.dot(front[2].reshape(-1, channel_count).T, grad_proj_b, preferred_element_type=jnp.float32)
    grad_normed = jnp.dot(grad_proj_b, proj_w.T, preferred_element_type=jnp.float32).reshape(upstream.shape)
    grad_pair = (upstream.astype(jnp.float32) + norm_back(front[0], front[1], grad_normed)).astype(jnp.bfloat16)
    return (grad_pair, grad_proj_w)

def ref_multiply(left_full, right_full, outgoing):
    pattern = 'cik,cjk->cij' if outgoing else 'cki,ckj->cij'
    result = jnp.einsum(pattern, left_full.astype(jnp.float32), right_full.astype(jnp.float32), precision=lax.Precision.HIGHEST)
    return result.astype(jnp.bfloat16)

def ref_edge_grads(gradient, left_full, right_full, outgoing):
    if outgoing:
        left_pattern, right_pattern = ('cij,cjk->cik', 'cij,cik->cjk')
    else:
        left_pattern, right_pattern = ('cij,ckj->cki', 'cij,cki->ckj')
    grad_f = gradient.astype(jnp.float32)
    grad_left = jnp.einsum(left_pattern, grad_f, right_full.astype(jnp.float32), precision=lax.Precision.HIGHEST)
    grad_right = jnp.einsum(right_pattern, grad_f, left_full.astype(jnp.float32), precision=lax.Precision.HIGHEST)
    return (grad_left.astype(jnp.bfloat16), grad_right.astype(jnp.bfloat16))

def to_channels(stacked):
    block_count, channel_count, block_rows, column_count = stacked.shape
    return jnp.moveaxis(stacked, 0, 1).reshape(channel_count, block_count * block_rows, column_count)

def tri_forward(pair_full, live, proj_w, out_w, outgoing):
    total = pair_full.shape[0]
    channel_count = pair_full.shape[2]
    block_rows = math.gcd(total, 64)
    block_count = total // block_rows
    pair_blocks = pair_full.reshape(block_count, block_rows, total, channel_count)
    live_blocks = live.reshape(block_count, block_rows)

    def make_edges(carried):
        front = front_values(carried[0], carried[1], live, proj_w)
        return (front[5].transpose(2, 0, 1).astype(jnp.bfloat16), front[6].transpose(2, 0, 1).astype(jnp.bfloat16))
    left_stack, right_stack = lax.map(make_edges, (pair_blocks, live_blocks))
    left_full = to_channels(left_stack)
    right_full = to_channels(right_stack)
    product = ref_multiply(left_full, right_full, outgoing).transpose(1, 2, 0)
    product_blocks = product.reshape(block_count, block_rows, total, channel_count)

    def finish(carried):
        front = front_values(carried[0], carried[1], live, proj_w)
        return rear_values(carried[0], carried[2], front[7], out_w)[4]
    new_pair = lax.map(finish, (pair_blocks, live_blocks, product_blocks)).reshape(total, total, channel_count)
    return (new_pair, product, left_full, right_full)

def tri_backward(upstream, pair_full, product, left_full, right_full, live, proj_w, out_w, outgoing):
    total = pair_full.shape[0]
    channel_count = pair_full.shape[2]
    block_rows = math.gcd(total, 64)
    block_count = total // block_rows
    shape_four = (block_count, block_rows, total, channel_count)
    pair_blocks = pair_full.reshape(shape_four)
    live_blocks = live.reshape(block_count, block_rows)
    product_blocks = product.reshape(shape_four)
    upstream_blocks = upstream.reshape(shape_four)

    def first_pass(carried):
        front = front_values(carried[0], carried[1], live, proj_w)
        rear = rear_values(carried[0], carried[2], front[7], out_w)
        grad_gate, grad_product, grad_out_w = rear_back(carried[3], front[7], out_w, rear)
        return (grad_product.transpose(2, 0, 1), grad_out_w)
    grad_stack, out_parts = lax.map(first_pass, (pair_blocks, live_blocks, product_blocks, upstream_blocks))
    grad_left_full, grad_right_full = ref_edge_grads(to_channels(grad_stack), left_full, right_full, outgoing)
    grad_left_blocks = grad_left_full.transpose(1, 2, 0).reshape(shape_four)
    grad_right_blocks = grad_right_full.transpose(1, 2, 0).reshape(shape_four)

    def second_pass(carried):
        front = front_values(carried[0], carried[1], live, proj_w)
        rear = rear_values(carried[0], carried[2], front[7], out_w)
        grad_gate = rear_back(carried[3], front[7], out_w, rear)[0]
        return front_back(carried[3], carried[4], carried[5], grad_gate, front, proj_w)
    grad_pair, proj_parts = lax.map(second_pass, (pair_blocks, live_blocks, product_blocks, upstream_blocks, grad_left_blocks, grad_right_blocks))
    return (grad_pair.reshape(total, total, channel_count), lax.optimization_barrier(jnp.sum(proj_parts, axis=0)), lax.optimization_barrier(jnp.sum(out_parts, axis=0)))

def reference(pair_in, residue_mask, chain_index, chain_bias, proj_weight, out_weight, cotangent):

    def complex_grads(carried):
        pair_full, mask_ints, chains, upstream = carried
        live = mask_ints.astype(jnp.float32)
        same_chain = (chains[:, None] == chains[None, :]).astype(jnp.float32)
        start_pair = (pair_full.astype(jnp.float32) + same_chain[:, :, None] * chain_bias).astype(jnp.bfloat16)
        middle_pair, prod_one, left_one, right_one = tri_forward(start_pair, live, proj_weight[0], out_weight[0], True)
        final_pair, prod_two, left_two, right_two = tri_forward(middle_pair, live, proj_weight[1], out_weight[1], False)
        grad_middle, proj_two, out_two = tri_backward(upstream, middle_pair, prod_two, left_two, right_two, live, proj_weight[1], out_weight[1], False)
        grad_start, proj_one, out_one = tri_backward(grad_middle, start_pair, prod_one, left_one, right_one, live, proj_weight[0], out_weight[0], True)
        chain_part = lax.optimization_barrier(jnp.sum(same_chain[:, :, None] * grad_start.astype(jnp.float32), axis=(0, 1)))
        return (final_pair, grad_start, jnp.stack([proj_one, proj_two]), jnp.stack([out_one, out_two]), chain_part)
    results = lax.map(complex_grads, (pair_in, residue_mask, chain_index, cotangent))
    inverse_count = 1.0 / (MEMBERS * NRES)
    return (results[0], results[1], lax.optimization_barrier(jnp.sum(results[2], axis=0)) * inverse_count, lax.optimization_barrier(jnp.sum(results[3], axis=0)) * inverse_count, lax.optimization_barrier(jnp.sum(results[4], axis=0)) * inverse_count)
```

```python
import functools

import jax
import jax.numpy as jnp
from jax import lax
from jax.experimental import pallas as pl
from jax.experimental.pallas import tpu as pltpu
from jax.sharding import PartitionSpec as P

EPSILON = 1e-05
MESH = pl.DeviceIdType.MESH
F32 = jnp.float32
BF16 = jnp.bfloat16
ROWS = 8
CH = 128
BLOCK = 32

L1, R1, P1, L2, R2, P2, DP2, DL2, DR2, DP1, DL1, DR1 = range(12)


def nt(a, b):
    return lax.dot_general(a, b, (((1,), (1,)), ((), ())), preferred_element_type=F32)


def tn(a, b):
    return lax.dot_general(a, b, (((0,), (0,)), ((), ())), preferred_element_type=F32)


def nn(a, b):
    return jnp.dot(a, b, preferred_element_type=F32)


def one_hot(rows, columns, wanted):
    r = lax.broadcasted_iota(jnp.int32, (rows, columns), 0)
    q = lax.broadcasted_iota(jnp.int32, (rows, columns), 1)
    return jnp.where(wanted(r, q), 1.0, 0.0).astype(F32)


def sigmoid(x):
    return 0.5 * jnp.tanh(0.5 * x) + 0.5


def norm(x):
    centred = x - jnp.mean(x, axis=0, keepdims=True)
    inv = lax.rsqrt(jnp.mean(centred * centred, axis=0, keepdims=True) + EPSILON)
    return centred * inv, inv


def norm_back(normed, inv, g):
    first = jnp.mean(g, axis=0, keepdims=True)
    second = jnp.mean(g * normed, axis=0, keepdims=True)
    return (g - first - normed * second) * inv


def kernel(
    n, dp, pair_ref, mask_ref, chain_ref, bias_ref, pw_ref, ow_ref, cot_ref,
    out_ref, pg_ref, gproj_ref, gout_ref, gchain_ref,
    eye_s, eyek_s, pf_s, pt_s, pwt_s, owt_s, bias_s, pm_s, sc_s,
    z_s, cot_s, dz_s, nb_s, nrm_s, istd_s, side_s, gate_s, pn_s, pnb_s, pstd_s, upd_s,
    dupd_s, dproj_s, edge_s, in_s, mats_s, chain_s,
    send, recv, g_s, rs_s, dpx_s, dpr_s, red_s, ag_s,
    send_sem, recv_sem, gsend_sem, grecv_sem,
):
    width = n * ROWS
    group = CH // n
    rows = group * ROWS
    per = BLOCK * ROWS // rows
    blocks = CH // BLOCK
    me = lax.axis_index("dap")
    mine = lax.axis_index("dp")

    barrier = pltpu.get_barrier_semaphore()

    def greet(t, carry):
        pl.semaphore_signal(barrier, inc=1, device_id={"dap": lax.rem(me + t, n)}, device_id_type=MESH)
        return carry

    lax.fori_loop(1, n, greet, 0)

    def greet_dp(t, carry):
        pl.semaphore_signal(barrier, inc=1, device_id={"dp": lax.rem(mine + t, dp)}, device_id_type=MESH)
        return carry

    lax.fori_loop(1, dp, greet_dp, 0)

    eye_s[...] = one_hot(CH, CH, lambda r, q: r == q).astype(BF16)
    eyek_s[...] = one_hot(width, width, lambda r, q: r == q).astype(BF16)
    pf_s[...] = one_hot(256, 256, lambda r, q: q == (r % ROWS) * BLOCK + r // ROWS).astype(BF16)
    pt_s[...] = one_hot(256, 256, lambda r, q: q == (r % BLOCK) * ROWS + r // BLOCK).astype(BF16)
    diag = one_hot(CH, CH, lambda r, q: r == q)
    bias_s[...] = jnp.sum(diag * bias_ref[...], axis=1, keepdims=True)
    eye = eye_s[...]
    for t in range(2):
        for b in range(5):
            pwt_s[t, b * CH:(b + 1) * CH, :] = nt(eye, pw_ref[t, :, b * CH:(b + 1) * CH]).astype(BF16)
        owt_s[t] = nt(eye, ow_ref[t]).astype(BF16)
    live = mask_ref[...].astype(F32)
    chain = chain_ref[...].astype(F32)
    own = one_hot(ROWS, width, lambda r, q: q == r + ROWS * me)
    pm_s[...] = jnp.sum(own * live, axis=1, keepdims=True) * live
    sc_s[...] = jnp.where(jnp.sum(own * chain, axis=1, keepdims=True) == chain, 1.0, 0.0)

    def partner_of(t):
        y, z, x = me // 8, (me // 4) % 2, me % 4
        ny, nz, nx = (y + t // 8) % 4, (z + (t // 4) % 2) % 2, (x + t % 4) % 4
        return (ny * 2 + nz) * 4 + nx if n == 32 else (me + t) % n

    def start_exchange(a):
        recv[a, pl.ds(me, 1)] = send[a, pl.ds(me, 1)]

        def go(t, carry):
            to = partner_of((t * 11) % n)
            pltpu.make_async_remote_copy(
                src_ref=send.at[a, to], dst_ref=recv.at[a, me],
                send_sem=send_sem.at[a], recv_sem=recv_sem.at[a],
                device_id={"dap": to}, device_id_type=MESH,
            ).start()
            return carry

        lax.fori_loop(1, n, go, 0)

    def whole(a):
        return pltpu.make_async_remote_copy(
            src_ref=send.at[a, pl.ds(0, n - 1)], dst_ref=recv.at[a, pl.ds(0, n - 1)],
            send_sem=send_sem.at[a], recv_sem=recv_sem.at[a],
            device_id={"dap": lax.rem(me + 1, n)}, device_id_type=MESH,
        )

    def pack(a, e):
        def step(b, carry):
            x = edge_s[e, :, pl.ds(b * BLOCK, BLOCK), :].reshape(256, width)
            y = nn(pf_s[...], x).astype(BF16)
            send[a, pl.ds(b * per, per)] = y.reshape(per, rows, width)
            return carry

        lax.fori_loop(0, blocks, step, 0)

    def unpack(a, e):
        def step(b, carry):
            x = recv[a, pl.ds(b * per, per)].reshape(256, width)
            in_s[e, :, pl.ds(b * BLOCK, BLOCK), :] = nn(pt_s[...], x).reshape(ROWS, BLOCK, width)
            return carry

        lax.fori_loop(0, blocks, step, 0)

    def channel_pair(a, cp):
        x = recv[a, :, pl.ds(cp * 16, 16), :].astype(F32).reshape(n, 2, ROWS, width)
        return [x[:, h].reshape(width, width).astype(BF16) for h in range(2)]

    def send_pair(a, cp, items):
        x = jnp.concatenate([item.reshape(n, ROWS, width) for item in items], axis=1)
        send[a, :, pl.ds(cp * 16, 16), :] = x.astype(BF16)

    def triangle(t, la, ra, pa):
        def step(cp, carry):
            left, right = channel_pair(la, cp), channel_pair(ra, cp)
            items = []
            for h in range(2):
                mats_s[t, 0, 2 * cp + h] = left[h]
                mats_s[t, 1, 2 * cp + h] = right[h]
                items.append(nt(left[h], right[h]) if t == 0 else tn(left[h], right[h]))
            send_pair(pa, cp, items)
            return carry

        lax.fori_loop(0, group // 2, step, 0)

    def triangle_back(t, da, la, ra):
        def step(cp, carry):
            grads = channel_pair(da, cp)
            dl, dr = [], []
            for h in range(2):
                left, right = mats_s[t, 0, 2 * cp + h], mats_s[t, 1, 2 * cp + h]
                if t == 0:
                    dl.append(nn(grads[h], right))
                    dr.append(tn(grads[h], left))
                else:
                    dl.append(nt(right, grads[h]))
                    dr.append(nn(left, grads[h]))
            send_pair(la, cp, dl)
            send_pair(ra, cp, dr)
            return carry

        lax.fori_loop(0, group // 2, step, 0)

    def front(t, i, z):
        normed, inv = norm(z.astype(F32))
        nb = normed.astype(BF16)
        nrm_s[t, i], istd_s[t, i], nb_s[t, i] = normed, inv, nb
        pm = pm_s[pl.ds(i, 1), :]
        for e in range(2):
            value = nn(pwt_s[t, 2 * e * CH:(2 * e + 1) * CH, :], nb)
            scale = pm * sigmoid(nn(pwt_s[t, (2 * e + 1) * CH:(2 * e + 2) * CH, :], nb))
            edge = scale * value
            side_s[t, 2 * e, i] = scale
            side_s[t, 2 * e + 1, i] = edge
            edge_s[e, i] = edge.astype(BF16)

    def gates(t):
        def step(i, carry):
            gate_s[t, i] = sigmoid(nn(pwt_s[t, 4 * CH:5 * CH, :], nb_s[t, i]))
            return carry

        lax.fori_loop(0, ROWS, step, 0)

    def rear(t, i):
        normed, inv = norm(in_s[0, i])
        nb = normed.astype(BF16)
        update = nn(owt_s[t], nb)
        pn_s[t, i], pstd_s[t, i], pnb_s[t, i], upd_s[t, i] = normed, inv, nb, update
        return (z_s[t, i].astype(F32) + gate_s[t, i] * update).astype(BF16)

    def rear_back(t, i, up):
        gate = gate_s[t, i]
        dupd = (up * gate).astype(BF16)
        dupd_s[i] = dupd
        dproj_s[4, i] = (up * upd_s[t, i] * gate * (1.0 - gate)).astype(BF16)
        g = nn(ow_ref[t], dupd)
        edge_s[0, i] = norm_back(pn_s[t, i], pstd_s[t, i], g).astype(BF16)

    def front_back(t, i, up):
        h = nn(pw_ref[t, :, 4 * CH:5 * CH], dproj_s[4, i])
        for e in range(2):
            grad, scale = in_s[e, i], side_s[t, 2 * e, i]
            first = (grad * scale).astype(BF16)
            second = (grad * side_s[t, 2 * e + 1, i] * (1.0 - scale)).astype(BF16)
            dproj_s[2 * e, i], dproj_s[2 * e + 1, i] = first, second
            h += nn(pw_ref[t, :, 2 * e * CH:(2 * e + 1) * CH], first)
            h += nn(pw_ref[t, :, (2 * e + 1) * CH:(2 * e + 2) * CH], second)
        return (up + norm_back(nrm_s[t, i], istd_s[t, i], h)).astype(BF16)

    def put_grad(t, b, value):
        g_rows = CH * 6 // n
        if CH % g_rows == 0:
            count = CH // g_rows
            g_s[t, b * count:(b + 1) * count, 0:g_rows, :] = value.reshape(count, g_rows, CH)
        else:
            at = b * CH
            done = 0
            while done < CH:
                piece, offset = divmod(at + done, g_rows)
                size = min(g_rows - offset, CH - done)
                g_s[t, piece, offset:offset + size, :] = value[done:done + size]
                done += size

    def out_grad(t):
        total = nt(pnb_s[t, 0], dupd_s[0])
        for i in range(1, ROWS):
            total += nt(pnb_s[t, i], dupd_s[i])
        put_grad(t, 5, total)

    def proj_grad(t, b):
        total = nt(nb_s[t, 0], dproj_s[b, 0])
        for i in range(1, ROWS):
            total += nt(nb_s[t, i], dproj_s[b, i])
        put_grad(t, b, total)

    def start_scatter(t):
        rs_s[t, pl.ds(me, 1)] = g_s[t, pl.ds(me, 1)]

        def go(k, carry):
            to = partner_of((k * 11) % n)
            pltpu.make_async_remote_copy(
                src_ref=g_s.at[t, to], dst_ref=rs_s.at[t, me],
                send_sem=gsend_sem.at[t, 0], recv_sem=grecv_sem.at[t, 0],
                device_id={"dap": to}, device_id_type=MESH,
            ).start()
            return carry

        lax.fori_loop(1, n, go, 0)

    def whole_scatter(t):
        return pltpu.make_async_remote_copy(
            src_ref=g_s.at[t, pl.ds(0, n - 1)], dst_ref=rs_s.at[t, pl.ds(0, n - 1)],
            send_sem=gsend_sem.at[t, 0], recv_sem=grecv_sem.at[t, 0],
            device_id={"dap": lax.rem(me + 1, n)}, device_id_type=MESH,
        )

    def start_across(t):
        whole_scatter(t).wait_recv()
        total = rs_s[t, 0]
        for k in range(1, n):
            total += rs_s[t, k]
        dpx_s[t] = total
        dpr_s[t, mine] = total

        def go(k, carry):
            pltpu.make_async_remote_copy(
                src_ref=dpx_s.at[t], dst_ref=dpr_s.at[t, mine],
                send_sem=gsend_sem.at[t, 1], recv_sem=grecv_sem.at[t, 1],
                device_id={"dp": lax.rem(mine + k, dp)}, device_id_type=MESH,
            ).start()
            return carry

        lax.fori_loop(1, dp, go, 0)

    def whole_across(t):
        return pltpu.make_async_remote_copy(
            src_ref=dpr_s.at[t, pl.ds(0, dp - 1)], dst_ref=dpr_s.at[t, pl.ds(0, dp - 1)],
            send_sem=gsend_sem.at[t, 1], recv_sem=grecv_sem.at[t, 1],
            device_id={"dp": lax.rem(mine + 1, dp)}, device_id_type=MESH,
        )

    def start_gather(t):
        whole_across(t).wait_recv()
        total = dpr_s[t, 0]
        for k in range(1, dp):
            total += dpr_s[t, k]
        total = total * (1.0 / (dp * width))
        red_s[t] = total
        ag_s[t, me] = total

        def go(k, carry):
            to = partner_of((k * 11) % n)
            pltpu.make_async_remote_copy(
                src_ref=red_s.at[t], dst_ref=ag_s.at[t, me],
                send_sem=gsend_sem.at[t, 2], recv_sem=grecv_sem.at[t, 2],
                device_id={"dap": to}, device_id_type=MESH,
            ).start()
            return carry

        lax.fori_loop(1, n, go, 0)

    def whole_gather(t):
        return pltpu.make_async_remote_copy(
            src_ref=ag_s.at[t, pl.ds(0, n - 1)], dst_ref=ag_s.at[t, pl.ds(0, n - 1)],
            send_sem=gsend_sem.at[t, 2], recv_sem=grecv_sem.at[t, 2],
            device_id={"dap": lax.rem(me + 1, n)}, device_id_type=MESH,
        )

    def finish_grad(t):
        whole_gather(t).wait_recv()
        g_rows = CH * 6 // n
        full = ag_s[t][:, 0:g_rows, :].reshape(6 * CH, CH)
        for b in range(5):
            gproj_ref[t, :, b * CH:(b + 1) * CH] = full[b * CH:(b + 1) * CH]
        gout_ref[t] = full[5 * CH:]

    def loop(body):
        def step(i, carry):
            body(i)
            return carry

        lax.fori_loop(0, ROWS, step, 0)

    def begin(i):
        x = nt(eye_s[...], pair_ref[i])
        z = (x + sc_s[pl.ds(i, 1), :] * bias_s[...]).astype(BF16)
        z_s[0, i] = z
        front(0, i, z)

    loop(begin)
    pack(L1, 0)
    pl.semaphore_wait(barrier, n - 1 + dp - 1)
    start_exchange(L1)
    pack(R1, 1)
    start_exchange(R1)
    gates(0)

    def turn(i):
        cot_s[i] = nt(eye_s[...], cot_ref[i]).astype(BF16)

    loop(turn)
    whole(L1).wait_recv()
    whole(R1).wait_recv()
    triangle(0, L1, R1, P1)
    start_exchange(P1)
    whole(P1).wait_recv()
    unpack(P1, 0)

    def middle(i):
        z = rear(0, i)
        z_s[1, i] = z
        front(1, i, z)

    loop(middle)
    pack(L2, 0)
    start_exchange(L2)
    pack(R2, 1)
    start_exchange(R2)
    gates(1)
    whole(L2).wait_recv()
    whole(R2).wait_recv()
    triangle(1, L2, R2, P2)
    start_exchange(P2)
    whole(P2).wait_recv()
    unpack(P2, 0)

    def last(i):
        z_s[2, i] = rear(1, i)
        rear_back(1, i, cot_s[i].astype(F32))

    loop(last)
    pack(DP2, 0)
    start_exchange(DP2)

    def write_out(i):
        out_ref[i] = nt(eyek_s[...], z_s[2, i]).astype(BF16)

    loop(write_out)
    out_grad(1)
    whole(DP2).wait_recv()
    triangle_back(1, DP2, DL2, DR2)
    start_exchange(DL2)
    start_exchange(DR2)
    whole(DL2).wait_recv()
    unpack(DL2, 0)
    whole(DR2).wait_recv()
    unpack(DR2, 1)

    def back(i):
        dz_s[0, i] = front_back(1, i, cot_s[i].astype(F32))

    loop(back)
    for b in range(5):
        proj_grad(1, b)
    g_s[1, :, CH * 6 // n:, :] = jnp.zeros((n, 8, CH), F32)

    def again(i):
        rear_back(0, i, dz_s[0, i].astype(F32))

    loop(again)
    pack(DP1, 0)
    start_exchange(DP1)
    start_scatter(1)
    out_grad(0)
    whole(DP1).wait_recv()
    triangle_back(0, DP1, DL1, DR1)
    start_exchange(DL1)
    start_exchange(DR1)
    start_across(1)
    start_gather(1)
    whole(DL1).wait_recv()
    unpack(DL1, 0)
    whole(DR1).wait_recv()
    unpack(DR1, 1)
    chain_s[...] = jnp.zeros_like(chain_s)

    def end(i):
        grad = front_back(0, i, dz_s[0, i].astype(F32))
        dz_s[1, i] = grad
        chain_s[...] += grad.astype(F32) * sc_s[pl.ds(i, 1), :]

    loop(end)
    for b in range(5):
        proj_grad(0, b)
    column = jnp.sum(chain_s[...], axis=1, keepdims=True)
    row = jnp.sum(diag * column, axis=0, keepdims=True)
    g_s[0, :, CH * 6 // n:, :] = jnp.broadcast_to(row[None], (n, 8, CH))
    start_scatter(0)

    def write_grad(i):
        pg_ref[i] = nt(eyek_s[...], dz_s[1, i]).astype(BF16)

    loop(write_grad)
    finish_grad(1)
    start_across(0)
    start_gather(0)
    gchain_ref[...] = red_s[0, CH * 6 // n:CH * 6 // n + 1, :]
    finish_grad(0)

    def drain(a, carry):
        whole(a).wait_send()
        return carry

    lax.fori_loop(0, 12, drain, 0)
    for t in range(2):
        whole_scatter(t).wait_send()
        whole_across(t).wait_send()
        whole_gather(t).wait_send()


def body(n, dp, pair_in, residue_mask, chain_index, chain_bias, proj_weight, out_weight, cotangent):
    width = n * ROWS
    group = CH // n
    grad_rows = CH * 6 // n + 8
    tensor = (ROWS, CH, width)
    vmem = pl.BlockSpec(memory_space=pltpu.VMEM)
    shapes = [
        jax.ShapeDtypeStruct((ROWS, width, CH), BF16),
        jax.ShapeDtypeStruct((ROWS, width, CH), BF16),
        jax.ShapeDtypeStruct((2, CH, 5 * CH), F32),
        jax.ShapeDtypeStruct((2, CH, CH), F32),
        jax.ShapeDtypeStruct((1, CH), F32),
    ]
    scratch = [
        pltpu.VMEM((CH, CH), BF16),
        pltpu.VMEM((width, width), BF16),
        pltpu.VMEM((256, 256), BF16),
        pltpu.VMEM((256, 256), BF16),
        pltpu.VMEM((2, 5 * CH, CH), BF16),
        pltpu.VMEM((2, CH, CH), BF16),
        pltpu.VMEM((CH, 1), F32),
        pltpu.VMEM((ROWS, width), F32),
        pltpu.VMEM((ROWS, width), F32),
        pltpu.VMEM((3,) + tensor, BF16),
        pltpu.VMEM(tensor, BF16),
        pltpu.VMEM((2,) + tensor, BF16),
        pltpu.VMEM((2,) + tensor, BF16),
        pltpu.VMEM((2,) + tensor, F32),
        pltpu.VMEM((2, ROWS, 1, width), F32),
        pltpu.VMEM((2, 4) + tensor, F32),
        pltpu.VMEM((2,) + tensor, F32),
        pltpu.VMEM((2,) + tensor, F32),
        pltpu.VMEM((2,) + tensor, BF16),
        pltpu.VMEM((2, ROWS, 1, width), F32),
        pltpu.VMEM((2,) + tensor, F32),
        pltpu.VMEM(tensor, BF16),
        pltpu.VMEM((5,) + tensor, BF16),
        pltpu.VMEM((2,) + tensor, BF16),
        pltpu.VMEM((2,) + tensor, F32),
        pltpu.VMEM((2, 2, group, width, width), BF16),
        pltpu.VMEM((CH, width), F32),
        pltpu.VMEM((12, n, group * ROWS, width), BF16),
        pltpu.VMEM((12, n, group * ROWS, width), BF16),
        pltpu.VMEM((2, n, grad_rows, CH), F32),
        pltpu.VMEM((2, n, grad_rows, CH), F32),
        pltpu.VMEM((2, grad_rows, CH), F32),
        pltpu.VMEM((2, dp, grad_rows, CH), F32),
        pltpu.VMEM((2, grad_rows, CH), F32),
        pltpu.VMEM((2, n, grad_rows, CH), F32),
        pltpu.SemaphoreType.DMA((12,)),
        pltpu.SemaphoreType.DMA((12,)),
        pltpu.SemaphoreType.DMA((2, 3)),
        pltpu.SemaphoreType.DMA((2, 3)),
    ]
    out_pair, pair_grad, grad_proj, grad_out, grad_chain = pl.pallas_call(
        functools.partial(kernel, n, dp),
        out_shape=shapes,
        in_specs=[vmem] * 7,
        out_specs=[vmem] * 5,
        scratch_shapes=scratch,
        compiler_params=pltpu.CompilerParams(
            collective_id=0, has_side_effects=True, vmem_limit_bytes=60 * 1024 * 1024
        ),
    )(
        pair_in[0], residue_mask, chain_index, chain_bias.reshape(1, CH),
        proj_weight, out_weight, cotangent[0],
    )
    return out_pair[None], pair_grad[None], grad_proj, grad_out, grad_chain.reshape(CH)


def solution(mesh):
    n, dp = mesh.shape["dap"], mesh.shape["dp"]
    rows = P("dp", "dap", None, None)
    return jax.shard_map(
        functools.partial(body, n, dp),
        mesh=mesh,
        in_specs=(rows, P("dp", None), P("dp", None), P(), P(), P(), rows),
        out_specs=(rows, rows, P(), P(), P()),
        check_vma=False,
    )
```

```python
import functools

import jax
import jax.numpy as jnp
from jax import lax
from jax.experimental import pallas as pl
from jax.experimental.pallas import tpu as pltpu
from jax.sharding import PartitionSpec as P

EPSILON = 1e-05
MESH = pl.DeviceIdType.MESH
F32 = jnp.float32
BF16 = jnp.bfloat16
ROWS = 8
CH = 128
BLOCK = 32

L1, R1, P1, L2, R2, P2, DP2, DL2, DR2, DP1, DL1, DR1 = range(12)


def nt(a, b):
    return lax.dot_general(a, b, (((1,), (1,)), ((), ())), preferred_element_type=F32)


def tn(a, b):
    return lax.dot_general(a, b, (((0,), (0,)), ((), ())), preferred_element_type=F32)


def nn(a, b):
    return jnp.dot(a, b, preferred_element_type=F32)


def one_hot(rows, columns, wanted):
    r = lax.broadcasted_iota(jnp.int32, (rows, columns), 0)
    q = lax.broadcasted_iota(jnp.int32, (rows, columns), 1)
    return jnp.where(wanted(r, q), 1.0, 0.0).astype(F32)


def sigmoid(x):
    return 0.5 * jnp.tanh(0.5 * x) + 0.5


def norm(x):
    centred = x - jnp.mean(x, axis=0, keepdims=True)
    inv = lax.rsqrt(jnp.mean(centred * centred, axis=0, keepdims=True) + EPSILON)
    return centred * inv, inv


def norm_back(normed, inv, g):
    first = jnp.mean(g, axis=0, keepdims=True)
    second = jnp.mean(g * normed, axis=0, keepdims=True)
    return (g - first - normed * second) * inv


def kernel(
    n, dp, pair_ref, mask_ref, chain_ref, bias_ref, pw_ref, ow_ref, cot_ref,
    out_ref, pg_ref, gproj_ref, gout_ref, gchain_ref,
    eye_s, pf_s, pt_s, pwt_s, owt_s, bias_s, pm_s, sc_s,
    z_s, cot_s, dz_s, nb_s, nrm_s, istd_s, side_s, gate_s, pn_s, pnb_s, pstd_s, upd_s,
    dupd_s, dproj_s, edge_s, in_s, mats_s, chain_s, acc_s,
    send, recv, ge_s, re_s, ae_s, gf_s, rf_s, af_s, xe_s, ye_s, xf_s, yf_s, cg_s, cr_s, cx_s, cy_s,
    send_sem, recv_sem, gsend_sem, grecv_sem,
):
    width = n * ROWS
    half = width // 2
    group = CH // n
    rows = group * ROWS
    half_rows = rows // 2
    per = BLOCK * ROWS // rows
    blocks = CH // BLOCK
    me = lax.axis_index("dap")
    mine = lax.axis_index("dp")

    barrier = pltpu.get_barrier_semaphore()

    def greet(t, carry):
        pl.semaphore_signal(barrier, inc=1, device_id={"dap": lax.rem(me + t, n)}, device_id_type=MESH)
        return carry

    lax.fori_loop(1, n, greet, 0)

    def greet_dp(t, carry):
        pl.semaphore_signal(barrier, inc=1, device_id={"dp": lax.rem(mine + t, dp)}, device_id_type=MESH)
        return carry

    lax.fori_loop(1, dp, greet_dp, 0)

    eye_s[...] = one_hot(CH, CH, lambda r, q: r == q).astype(BF16)
    pf_s[...] = one_hot(256, 256, lambda r, q: q == (r % ROWS) * BLOCK + r // ROWS).astype(BF16)
    pt_s[...] = one_hot(256, 256, lambda r, q: q == (r % BLOCK) * ROWS + r // BLOCK).astype(BF16)
    diag = one_hot(CH, CH, lambda r, q: r == q)
    bias_s[...] = jnp.sum(diag * bias_ref[...], axis=1, keepdims=True)
    eye = eye_s[...]
    for t in range(2):
        for b in range(5):
            pwt_s[t, b * CH:(b + 1) * CH, :] = nt(eye, pw_ref[t, :, b * CH:(b + 1) * CH]).astype(BF16)
        owt_s[t] = nt(eye, ow_ref[t]).astype(BF16)
    live = mask_ref[...].astype(F32)
    chain = chain_ref[...].astype(F32)
    own = one_hot(ROWS, width, lambda r, q: q == r + ROWS * me)
    pair_mask = jnp.sum(own * live, axis=1, keepdims=True) * live
    same = jnp.where(jnp.sum(own * chain, axis=1, keepdims=True) == chain, 1.0, 0.0)
    for p in range(2):
        pm_s[p * ROWS:(p + 1) * ROWS, :] = pair_mask[:, p * half:(p + 1) * half]
        sc_s[p * ROWS:(p + 1) * ROWS, :] = same[:, p * half:(p + 1) * half]

    def partner_of(t):
        y, z, x = me // 8, (me // 4) % 2, me % 4
        ny, nz, nx = (y + t // 8) % 4, (z + (t // 4) % 2) % 2, (x + t % 4) % 4
        return (ny * 2 + nz) * 4 + nx if n == 32 else (me + t) % n

    def push(messages):
        for a, r0, rn, p, k in messages:
            at = (a, pl.ds(me, 1), slice(r0, r0 + rn), slice(p * half, (p + 1) * half))
            recv[at] = send[at]

        def go(t, carry):
            to = partner_of((t * 11) % n)
            for a, r0, rn, p, k in messages:
                part = (pl.ds(r0, rn), pl.ds(p * half, half))
                pltpu.make_async_remote_copy(
                    src_ref=send.at[(a, to) + part], dst_ref=recv.at[(a, me) + part],
                    send_sem=send_sem.at[a], recv_sem=recv_sem.at[a, k],
                    device_id={"dap": to}, device_id_type=MESH,
                ).start()
            return carry

        lax.fori_loop(1, n, go, 0)

    def arrived(a, r0, rn, p, k):
        part = (a, pl.ds(0, n - 1), pl.ds(r0, rn), pl.ds(p * half, half))
        pltpu.make_async_remote_copy(
            src_ref=send.at[part], dst_ref=recv.at[part],
            send_sem=send_sem.at[a], recv_sem=recv_sem.at[a, k],
            device_id={"dap": lax.rem(me + 1, n)}, device_id_type=MESH,
        ).wait_recv()

    def sent(a):
        part = (a, pl.ds(0, n - 1))
        pltpu.make_async_remote_copy(
            src_ref=send.at[part], dst_ref=recv.at[part],
            send_sem=send_sem.at[a], recv_sem=recv_sem.at[a, 0],
            device_id={"dap": lax.rem(me + 1, n)}, device_id_type=MESH,
        ).wait_send()

    def to_channels(p, items):
        if p == 0:
            push([(a, 0, rows, 0, 0) for a in items])
        else:
            push([(a, 0, half_rows, 1, 1) for a in items])
            push([(a, half_rows, half_rows, 1, 2) for a in items])

    def channels_here(cc, items):
        for a in items:
            if cc == 0:
                arrived(a, 0, rows, 0, 0)
            arrived(a, cc * half_rows, half_rows, 1, 1 + cc)

    def to_pairs(cc, items):
        push([(a, cc * half_rows, half_rows, 0, 0) for a in items])
        if cc == 1:
            push([(a, 0, rows, 1, 1) for a in items])

    def pairs_here(p, a):
        arrived(a, 0, rows, p, p)

    def pack(p, a, e):
        def step(b, carry):
            x = edge_s[e, p * ROWS:(p + 1) * ROWS, pl.ds(b * BLOCK, BLOCK), :].reshape(256, half)
            y = nn(pf_s[...], x).astype(BF16)
            send[a, pl.ds(b * per, per), :, p * half:(p + 1) * half] = y.reshape(per, rows, half)
            return carry

        lax.fori_loop(0, blocks, step, 0, unroll=4)

    def unpack(p, a, e):
        def step(b, carry):
            x = recv[a, pl.ds(b * per, per), :, p * half:(p + 1) * half].reshape(256, half)
            y = nn(pt_s[...], x).reshape(ROWS, BLOCK, half)
            in_s[e, p * ROWS:(p + 1) * ROWS, pl.ds(b * BLOCK, BLOCK), :] = y
            return carry

        lax.fori_loop(0, blocks, step, 0, unroll=4)

    def channel_pair(a, at):
        x = recv[a, :, at:at + 16, :].astype(F32).reshape(n, 2, ROWS, width)
        return [x[:, h].reshape(width, width).astype(BF16) for h in range(2)]

    def put_pair(a, at, items):
        x = jnp.concatenate([item.reshape(n, ROWS, width) for item in items], axis=1)
        send[a, :, at:at + 16, :] = x.astype(BF16)

    def triangle(t, la, ra, pa):
        for cc in range(2):
            channels_here(cc, (la, ra))
            for cp in range(cc * group // 4, (cc + 1) * group // 4):
                left, right = channel_pair(la, cp * 16), channel_pair(ra, cp * 16)
                items = []
                for h in range(2):
                    mats_s[t, 0, 2 * cp + h] = left[h]
                    mats_s[t, 1, 2 * cp + h] = right[h]
                    items.append(nt(left[h], right[h]) if t == 0 else tn(left[h], right[h]))
                put_pair(pa, cp * 16, items)
            to_pairs(cc, (pa,))

    def triangle_back(t, da, la, ra):
        for cc in range(2):
            channels_here(cc, (da,))
            for cp in range(cc * group // 4, (cc + 1) * group // 4):
                grads = channel_pair(da, cp * 16)
                dl, dr = [], []
                for h in range(2):
                    left, right = mats_s[t, 0, 2 * cp + h], mats_s[t, 1, 2 * cp + h]
                    if t == 0:
                        dl.append(nn(grads[h], right))
                        dr.append(tn(grads[h], left))
                    else:
                        dl.append(nt(right, grads[h]))
                        dr.append(nn(left, grads[h]))
                put_pair(la, cp * 16, dl)
                put_pair(ra, cp * 16, dr)
            to_pairs(cc, (la, ra))

    def front(t, q, z):
        normed, inv = norm(z.astype(F32))
        nb = normed.astype(BF16)
        nrm_s[t, q], istd_s[t, q], nb_s[t, q] = normed, inv, nb
        pm = pm_s[pl.ds(q, 1), :]
        for e in range(2):
            value = nn(pwt_s[t, 2 * e * CH:(2 * e + 1) * CH, :], nb)
            scale = pm * sigmoid(nn(pwt_s[t, (2 * e + 1) * CH:(2 * e + 2) * CH, :], nb))
            edge = scale * value
            side_s[t, 2 * e, q] = scale
            side_s[t, 2 * e + 1, q] = edge
            edge_s[e, q] = edge.astype(BF16)

    def gates(t):
        def step(q, carry):
            gate_s[t, q] = sigmoid(nn(pwt_s[t, 4 * CH:5 * CH, :], nb_s[t, q]))
            return carry

        lax.fori_loop(0, 2 * ROWS, step, 0, unroll=8)

    def rear(t, q):
        normed, inv = norm(in_s[0, q])
        nb = normed.astype(BF16)
        update = nn(owt_s[t], nb)
        pn_s[t, q], pstd_s[t, q], pnb_s[t, q], upd_s[t, q] = normed, inv, nb, update
        return (z_s[t, q].astype(F32) + gate_s[t, q] * update).astype(BF16)

    def rear_back(t, q, up):
        gate = gate_s[t, q]
        dupd = (up * gate).astype(BF16)
        dupd_s[t, q] = dupd
        dproj_s[t, 4, q] = (up * upd_s[t, q] * gate * (1.0 - gate)).astype(BF16)
        g = nn(ow_ref[t], dupd)
        edge_s[0, q] = norm_back(pn_s[t, q], pstd_s[t, q], g).astype(BF16)

    def front_back(t, q, up):
        h = nn(pw_ref[t, :, 4 * CH:5 * CH], dproj_s[t, 4, q])
        for e in range(2):
            grad, scale = in_s[e, q], side_s[t, 2 * e, q]
            first = (grad * scale).astype(BF16)
            second = (grad * side_s[t, 2 * e + 1, q] * (1.0 - scale)).astype(BF16)
            dproj_s[t, 2 * e, q], dproj_s[t, 2 * e + 1, q] = first, second
            h += nn(pw_ref[t, :, 2 * e * CH:(2 * e + 1) * CH], first)
            h += nn(pw_ref[t, :, (2 * e + 1) * CH:(2 * e + 2) * CH], second)
        return (up + norm_back(nrm_s[t, q], istd_s[t, q], h)).astype(BF16)

    early_rows, late_rows = 8 * CH // n, 4 * CH // n

    def out_grad(t):
        total = nt(pnb_s[t, 0], dupd_s[t, 0])
        for q in range(1, 2 * ROWS):
            total += nt(pnb_s[t, q], dupd_s[t, q])
        return total

    def proj_grad(t, b, p=None):
        first, last = (0, 2 * ROWS) if p is None else (p * ROWS, (p + 1) * ROWS)
        total = nt(nb_s[t, first], dproj_s[t, b, first])
        for q in range(first + 1, last):
            total += nt(nb_s[t, q], dproj_s[t, b, q])
        return total

    def piece(at, size):
        return pl.ds(pl.multiple_of(at * size, size), size)

    def scatter(g, r, size, k):
        r[pl.ds(me, 1)] = g[piece(me, size), :].reshape(1, size, CH)

        def go(t, carry):
            to = partner_of((t * 11) % n)
            pltpu.make_async_remote_copy(
                src_ref=g.at[piece(to, size)], dst_ref=r.at[me],
                send_sem=gsend_sem.at[k], recv_sem=grecv_sem.at[k],
                device_id={"dap": to}, device_id_type=MESH,
            ).start()
            return carry

        lax.fori_loop(1, n, go, 0)

    def spread(x, r, k):
        def go(t, carry):
            to = partner_of((t * 11) % n)
            pltpu.make_async_remote_copy(
                src_ref=x, dst_ref=r.at[me], send_sem=gsend_sem.at[k], recv_sem=grecv_sem.at[k],
                device_id={"dap": to}, device_id_type=MESH,
            ).start()
            return carry

        lax.fori_loop(1, n, go, 0)

    def across(x, y, k):
        y[mine] = x[...]

        def go(t, carry):
            pltpu.make_async_remote_copy(
                src_ref=x, dst_ref=y.at[mine], send_sem=gsend_sem.at[k], recv_sem=grecv_sem.at[k],
                device_id={"dp": lax.rem(mine + t, dp)}, device_id_type=MESH,
            ).start()
            return carry

        lax.fori_loop(1, dp, go, 0)

    def bulk(r, count, k):
        return pltpu.make_async_remote_copy(
            src_ref=r.at[pl.ds(0, count)], dst_ref=r.at[pl.ds(0, count)],
            send_sem=gsend_sem.at[k], recv_sem=grecv_sem.at[k],
            device_id={"dap": lax.rem(me + 1, n)}, device_id_type=MESH,
        )

    def summed(r, count):
        total = r[0].astype(F32)
        for t in range(1, count):
            total += r[t].astype(F32)
        return total

    inverse = 1.0 / (dp * width)

    def loop(body, p):
        def step(i, carry):
            body(i, i + p * ROWS)
            return carry

        lax.fori_loop(0, ROWS, step, 0, unroll=8)

    for p in range(2):
        def begin(i, q):
            x = nt(eye_s[...], pair_ref[i, p * half:(p + 1) * half, :])
            z = (x + sc_s[pl.ds(q, 1), :] * bias_s[...]).astype(BF16)
            z_s[0, q] = z
            front(0, q, z)

        loop(begin, p)
        pack(p, L1, 0)
        pack(p, R1, 1)
        if p == 0:
            pl.semaphore_wait(barrier, n - 1 + dp - 1)
        to_channels(p, (L1, R1))
    gates(0)
    for p in range(2):
        def turn(i, q):
            cot_s[q] = nt(eye_s[...], cot_ref[i, p * half:(p + 1) * half, :]).astype(BF16)

        loop(turn, p)
    triangle(0, L1, R1, P1)
    for p in range(2):
        def middle(i, q):
            z = rear(0, q)
            z_s[1, q] = z
            front(1, q, z)

        pairs_here(p, P1)
        unpack(p, P1, 0)
        loop(middle, p)
        pack(p, L2, 0)
        pack(p, R2, 1)
        to_channels(p, (L2, R2))
    gates(1)
    triangle(1, L2, R2, P2)

    for p in range(2):
        def last(i, q):
            z_s[2, q] = rear(1, q)
            rear_back(1, q, cot_s[q].astype(F32))

        pairs_here(p, P2)
        unpack(p, P2, 0)
        loop(last, p)
        pack(p, DP2, 0)
        to_channels(p, (DP2,))
    for p in range(2):
        def write_out(i, q):
            out_ref[i, p * half:(p + 1) * half, :] = nt(eye_s[0:half, 0:half], z_s[2, q]).astype(BF16)

        loop(write_out, p)
    ge_s[5 * CH:6 * CH, :] = out_grad(1).astype(BF16)
    triangle_back(1, DP2, DL2, DR2)
    ge_s[4 * CH:5 * CH, :] = proj_grad(1, 4).astype(BF16)

    for p in range(2):
        def back(i, q):
            grad = front_back(1, q, cot_s[q].astype(F32))
            dz_s[0, q] = grad
            rear_back(0, q, grad.astype(F32))

        pairs_here(p, DL2)
        unpack(p, DL2, 0)
        pairs_here(p, DR2)
        unpack(p, DR2, 1)
        loop(back, p)
        pack(p, DP1, 0)
        to_channels(p, (DP1,))
    for b in range(4):
        ge_s[b * CH:(b + 1) * CH, :] = proj_grad(1, b).astype(BF16)
    ge_s[6 * CH:7 * CH, :] = proj_grad(0, 4).astype(BF16)
    ge_s[7 * CH:8 * CH, :] = out_grad(0).astype(BF16)
    scatter(ge_s, re_s, early_rows, 0)
    triangle_back(0, DP1, DL1, DR1)
    bulk(re_s, n - 1, 0).wait_recv()
    xe_s[...] = summed(re_s, n)
    across(xe_s, ye_s, 1)
    chain_s[...] = jnp.zeros_like(chain_s)
    for p in range(2):
        def end(i, q):
            grad = front_back(0, q, dz_s[0, q].astype(F32))
            dz_s[1, q] = grad
            chain_s[...] += grad.astype(F32) * sc_s[pl.ds(q, 1), :]

        def write_grad(i, q):
            pg_ref[i, p * half:(p + 1) * half, :] = nt(eye_s[0:half, 0:half], dz_s[1, q]).astype(BF16)

        pairs_here(p, DL1)
        unpack(p, DL1, 0)
        pairs_here(p, DR1)
        unpack(p, DR1, 1)
        loop(end, p)
        for b in range(4):
            if p == 0:
                acc_s[b] = proj_grad(0, b, 0)
            else:
                gf_s[b * CH:(b + 1) * CH, :] = (acc_s[b] + proj_grad(0, b, 1)).astype(BF16)
        if p == 0:
            loop(write_grad, 0)
    scatter(gf_s, rf_s, late_rows, 3)
    column = jnp.sum(chain_s[...], axis=1, keepdims=True)
    cg_s[...] = jnp.sum(diag * column, axis=0, keepdims=True)
    cr_s[me] = cg_s[...]
    spread(cg_s, cr_s, 6)
    loop(write_grad, 1)

    bulk(ye_s, dp - 1, 1).wait_recv()
    ae_s[me] = (summed(ye_s, dp) * inverse).astype(BF16)
    spread(ae_s.at[me], ae_s, 2)
    bulk(rf_s, n - 1, 3).wait_recv()
    xf_s[...] = summed(rf_s, n)
    across(xf_s, yf_s, 4)
    bulk(cr_s, n - 1, 6).wait_recv()
    cx_s[...] = summed(cr_s, n)
    across(cx_s, cy_s, 7)
    bulk(yf_s, dp - 1, 4).wait_recv()
    af_s[me] = (summed(yf_s, dp) * inverse).astype(BF16)
    spread(af_s.at[me], af_s, 5)
    bulk(cy_s, dp - 1, 7).wait_recv()
    gchain_ref[...] = summed(cy_s, dp) * inverse
    bulk(ae_s, n - 1, 2).wait_recv()
    full = ae_s[...].reshape(8 * CH, CH).astype(F32)
    for b in range(5):
        gproj_ref[1, :, b * CH:(b + 1) * CH] = full[b * CH:(b + 1) * CH]
    gout_ref[1] = full[5 * CH:6 * CH]
    gproj_ref[0, :, 4 * CH:5 * CH] = full[6 * CH:7 * CH]
    gout_ref[0] = full[7 * CH:8 * CH]

    def drain(a, carry):
        sent(a)
        return carry

    lax.fori_loop(0, 12, drain, 0)
    for r, count, k in ((re_s, n, 0), (ye_s, dp, 1), (ae_s, n, 2), (rf_s, n, 3), (yf_s, dp, 4), (cr_s, n, 6), (cy_s, dp, 7)):
        bulk(r, count - 1, k).wait_send()
    bulk(af_s, n - 1, 5).wait_recv()
    full = af_s[...].reshape(4 * CH, CH).astype(F32)
    for b in range(4):
        gproj_ref[0, :, b * CH:(b + 1) * CH] = full[b * CH:(b + 1) * CH]
    bulk(af_s, n - 1, 5).wait_send()


def hand_over(*refs):
    count = (len(refs) - 2) // 3
    given, outs, held = refs[:count], refs[count:2 * count], refs[2 * count:3 * count]
    in_sem, out_sem = refs[-2:]
    fetched = [pltpu.make_async_copy(given[k], held[k], in_sem.at[k]) for k in range(count)]
    put = [pltpu.make_async_copy(held[k], outs[k], out_sem.at[k]) for k in range(count)]
    for copy in fetched:
        copy.start()
    for k in range(count):
        fetched[k].wait()
        put[k].start()
    for copy in put:
        copy.wait()


def body(n, dp, pair_in, residue_mask, chain_index, chain_bias, proj_weight, out_weight, cotangent):
    width = n * ROWS
    group = CH // n
    early_rows, late_rows = 8 * CH // n, 4 * CH // n
    tensor = (2 * ROWS, CH, width // 2)
    line = (2 * ROWS, 1, width // 2)
    vmem = pl.BlockSpec(memory_space=pltpu.VMEM)
    shapes = [
        jax.ShapeDtypeStruct((ROWS, width, CH), BF16),
        jax.ShapeDtypeStruct((ROWS, width, CH), BF16),
        jax.ShapeDtypeStruct((2, CH, 5 * CH), F32),
        jax.ShapeDtypeStruct((2, CH, CH), F32),
        jax.ShapeDtypeStruct((1, CH), F32),
    ]
    scratch = [
        pltpu.VMEM((CH, CH), BF16),
        pltpu.VMEM((256, 256), BF16),
        pltpu.VMEM((256, 256), BF16),
        pltpu.VMEM((2, 5 * CH, CH), BF16),
        pltpu.VMEM((2, CH, CH), BF16),
        pltpu.VMEM((CH, 1), F32),
        pltpu.VMEM((2 * ROWS, width // 2), F32),
        pltpu.VMEM((2 * ROWS, width // 2), F32),
        pltpu.VMEM((3,) + tensor, BF16),
        pltpu.VMEM(tensor, BF16),
        pltpu.VMEM((2,) + tensor, BF16),
        pltpu.VMEM((2,) + tensor, BF16),
        pltpu.VMEM((2,) + tensor, F32),
        pltpu.VMEM((2,) + line, F32),
        pltpu.VMEM((2, 4) + tensor, F32),
        pltpu.VMEM((2,) + tensor, F32),
        pltpu.VMEM((2,) + tensor, F32),
        pltpu.VMEM((2,) + tensor, BF16),
        pltpu.VMEM((2,) + line, F32),
        pltpu.VMEM((2,) + tensor, F32),
        pltpu.VMEM((2,) + tensor, BF16),
        pltpu.VMEM((2, 5) + tensor, BF16),
        pltpu.VMEM((2,) + tensor, BF16),
        pltpu.VMEM((2,) + tensor, F32),
        pltpu.VMEM((2, 2, group, width, width), BF16),
        pltpu.VMEM((CH, width // 2), F32),
        pltpu.VMEM((4, CH, CH), F32),
        pltpu.VMEM((12, n, group * ROWS, width), BF16),
        pltpu.VMEM((12, n, group * ROWS, width), BF16),
        pltpu.VMEM((8 * CH, CH), BF16),
        pltpu.VMEM((n, early_rows, CH), BF16),
        pltpu.VMEM((n, early_rows, CH), BF16),
        pltpu.VMEM((4 * CH, CH), BF16),
        pltpu.VMEM((n, late_rows, CH), BF16),
        pltpu.VMEM((n, late_rows, CH), BF16),
        pltpu.VMEM((early_rows, CH), F32),
        pltpu.VMEM((dp, early_rows, CH), F32),
        pltpu.VMEM((late_rows, CH), F32),
        pltpu.VMEM((dp, late_rows, CH), F32),
        pltpu.VMEM((1, CH), F32),
        pltpu.VMEM((n, 1, CH), F32),
        pltpu.VMEM((1, CH), F32),
        pltpu.VMEM((dp, 1, CH), F32),
        pltpu.SemaphoreType.DMA((12,)),
        pltpu.SemaphoreType.DMA((12, 3)),
        pltpu.SemaphoreType.DMA((8,)),
        pltpu.SemaphoreType.DMA((8,)),
    ]
    results = pl.pallas_call(
        functools.partial(kernel, n, dp),
        out_shape=shapes,
        in_specs=[vmem] * 7,
        out_specs=[vmem] * 5,
        scratch_shapes=scratch,
        compiler_params=pltpu.CompilerParams(
            collective_id=0, has_side_effects=True, vmem_limit_bytes=62 * 1024 * 1024
        ),
    )(
        pair_in[0], residue_mask, chain_index, chain_bias.reshape(1, CH),
        proj_weight, out_weight, cotangent[0],
    )
    anywhere = pl.BlockSpec(memory_space=pl.ANY)
    out_pair, pair_grad, grad_proj, grad_out, grad_chain = pl.pallas_call(
        hand_over,
        out_shape=shapes,
        in_specs=[anywhere] * 5,
        out_specs=[anywhere] * 5,
        scratch_shapes=[pltpu.VMEM(shape.shape, shape.dtype) for shape in shapes]
        + [pltpu.SemaphoreType.DMA((5,)), pltpu.SemaphoreType.DMA((5,))],
        compiler_params=pltpu.CompilerParams(vmem_limit_bytes=62 * 1024 * 1024),
    )(*results)
    return out_pair[None], pair_grad[None], grad_proj, grad_out, grad_chain.reshape(CH)


def solution(mesh):
    n, dp = mesh.shape["dap"], mesh.shape["dp"]
    rows = P("dp", "dap", None, None)
    return jax.shard_map(
        functools.partial(body, n, dp),
        mesh=mesh,
        in_specs=(rows, P("dp", None), P("dp", None), P(), P(), P(), rows),
        out_specs=(rows, rows, P(), P(), P()),
        check_vma=False,
    )
```

```python
import functools

import jax
import jax.numpy as jnp
from jax import lax
from jax.experimental import pallas as pl
from jax.experimental.pallas import tpu as pltpu
from jax.sharding import PartitionSpec as P

EPSILON = 1e-05
MESH = pl.DeviceIdType.MESH
F32 = jnp.float32
BF16 = jnp.bfloat16
ROWS = 8
CH = 128
BLOCK = 32

L1, R1, P1, L2, R2, P2, DP2, DL2, DR2, DP1, DL1, DR1 = range(12)


def nt(a, b):
    return lax.dot_general(a, b, (((1,), (1,)), ((), ())), preferred_element_type=F32)


def tn(a, b):
    return lax.dot_general(a, b, (((0,), (0,)), ((), ())), preferred_element_type=F32)


def nn(a, b):
    return jnp.dot(a, b, preferred_element_type=F32)


def one_hot(rows, columns, wanted):
    r = lax.broadcasted_iota(jnp.int32, (rows, columns), 0)
    q = lax.broadcasted_iota(jnp.int32, (rows, columns), 1)
    return jnp.where(wanted(r, q), 1.0, 0.0).astype(F32)


def sigmoid(x):
    return 0.5 * jnp.tanh(0.5 * x) + 0.5


def norm(x):
    centred = x - jnp.mean(x, axis=0, keepdims=True)
    inv = lax.rsqrt(jnp.mean(centred * centred, axis=0, keepdims=True) + EPSILON)
    return centred * inv, inv


def norm_back(normed, inv, g):
    first = jnp.mean(g, axis=0, keepdims=True)
    second = jnp.mean(g * normed, axis=0, keepdims=True)
    return (g - first - normed * second) * inv


def kernel(
    n, dp, pair_ref, mask_ref, chain_ref, bias_ref, pw_ref, ow_ref, cot_ref,
    out_ref, pg_ref, gproj_ref, gout_ref, gchain_ref,
    eye_s, pf_s, pt_s, pwt_s, owt_s, bias_s, pm_s, sc_s,
    z_s, cot_s, dz_s, nb_s, nrm_s, istd_s, side_s, gate_s, pn_s, pnb_s, pstd_s, upd_s,
    dupd_s, dproj_s, edge_s, in_s, mats_s, chain_s, acc_s,
    send, recv, ge_s, re_s, ae_s, gf_s, rf_s, af_s, xe_s, ye_s, xf_s, yf_s, cg_s, cr_s, cx_s, cy_s, outv_s, pgv_s,
    send_sem, recv_sem, gsend_sem, grecv_sem, put_sem,
):
    width = n * ROWS
    half = width // 2
    group = CH // n
    rows = group * ROWS
    half_rows = rows // 2
    per = BLOCK * ROWS // rows
    blocks = CH // BLOCK
    me = lax.axis_index("dap")
    mine = lax.axis_index("dp")

    barrier = pltpu.get_barrier_semaphore()

    def greet(t, carry):
        pl.semaphore_signal(barrier, inc=1, device_id={"dap": lax.rem(me + t, n)}, device_id_type=MESH)
        return carry

    lax.fori_loop(1, n, greet, 0)

    def greet_dp(t, carry):
        pl.semaphore_signal(barrier, inc=1, device_id={"dp": lax.rem(mine + t, dp)}, device_id_type=MESH)
        return carry

    lax.fori_loop(1, dp, greet_dp, 0)

    eye_s[...] = one_hot(CH, CH, lambda r, q: r == q).astype(BF16)
    pf_s[...] = one_hot(256, 256, lambda r, q: q == (r % ROWS) * BLOCK + r // ROWS).astype(BF16)
    diag = one_hot(CH, CH, lambda r, q: r == q)
    bias_s[...] = jnp.sum(diag * bias_ref[...], axis=1, keepdims=True)

    def turn_weight(t, b):
        pwt_s[t, b * CH:(b + 1) * CH, :] = nt(eye_s[...], pw_ref[t, :, b * CH:(b + 1) * CH]).astype(BF16)

    for b in range(4):
        turn_weight(0, b)
    live = mask_ref[...].astype(F32)
    chain = chain_ref[...].astype(F32)
    own = one_hot(ROWS, width, lambda r, q: q == r + ROWS * me)
    pair_mask = jnp.sum(own * live, axis=1, keepdims=True) * live
    same = jnp.where(jnp.sum(own * chain, axis=1, keepdims=True) == chain, 1.0, 0.0)
    for p in range(2):
        pm_s[p * ROWS:(p + 1) * ROWS, :] = pair_mask[:, p * half:(p + 1) * half]
        sc_s[p * ROWS:(p + 1) * ROWS, :] = same[:, p * half:(p + 1) * half]

    if n == 32:
        row, plane, column = me // 8, (me // 4) % 2, me % 4
        planes = [4 * lax.rem(plane + k, 2) for k in range(2)]
        columns = [lax.rem(column + k, 4) for k in range(4)]

    def to_all(start):
        if n != 32:
            lax.fori_loop(1, n, lambda t, carry: (start(lax.rem(me + t, n)), carry)[1], 0)
            return

        def some(turn, first):
            lines = [8 * lax.rem(row + turn + k, 4) for k in range(4)]
            for k in (1, 2, 3, 0):
                for h in (1, 0):
                    if not (first and k == 0 and h == 0):
                        start(lines[k] + planes[h] + columns[k])

        some(0, True)
        lax.fori_loop(1, 4, lambda turn, carry: (some(turn, False), carry)[1], 0)

    def push(messages):
        for a, r0, rn, p, k in messages:
            at = (a, pl.ds(me, 1), slice(r0, r0 + rn), slice(p * half, (p + 1) * half))
            recv[at] = send[at]

        def go(to):
            for a, r0, rn, p, k in messages:
                part = (pl.ds(r0, rn), pl.ds(p * half, half))
                pltpu.make_async_remote_copy(
                    src_ref=send.at[(a, to) + part], dst_ref=recv.at[(a, me) + part],
                    send_sem=send_sem.at[a], recv_sem=recv_sem.at[a, k],
                    device_id={"dap": to}, device_id_type=MESH,
                ).start()

        to_all(go)

    def arrived(a, r0, rn, p, k):
        part = (a, pl.ds(0, n - 1), pl.ds(r0, rn), pl.ds(p * half, half))
        pltpu.make_async_remote_copy(
            src_ref=send.at[part], dst_ref=recv.at[part],
            send_sem=send_sem.at[a], recv_sem=recv_sem.at[a, k],
            device_id={"dap": lax.rem(me + 1, n)}, device_id_type=MESH,
        ).wait_recv()

    def sent(a):
        part = (a, pl.ds(0, n - 1))
        pltpu.make_async_remote_copy(
            src_ref=send.at[part], dst_ref=recv.at[part],
            send_sem=send_sem.at[a], recv_sem=recv_sem.at[a, 0],
            device_id={"dap": lax.rem(me + 1, n)}, device_id_type=MESH,
        ).wait_send()

    def to_channels(p, items):
        if p == 0:
            push([(a, 0, rows, 0, 0) for a in items])
        else:
            push([(a, 0, half_rows, 1, 1) for a in items])
            push([(a, half_rows, half_rows, 1, 2) for a in items])

    def channels_here(cc, items):
        for a in items:
            if cc == 0:
                arrived(a, 0, rows, 0, 0)
            arrived(a, cc * half_rows, half_rows, 1, 1 + cc)

    def to_pairs(cc, items):
        push([(a, cc * half_rows, half_rows, 0, 0) for a in items])
        if cc == 1:
            push([(a, 0, rows, 1, 1) for a in items])

    def pairs_here(p, a):
        arrived(a, 0, rows, p, p)

    def pack(p, a, e):
        def step(b, carry):
            x = edge_s[e, p * ROWS:(p + 1) * ROWS, pl.ds(b * BLOCK, BLOCK), :].reshape(256, half)
            y = nn(pf_s[...], x).astype(BF16)
            send[a, pl.ds(b * per, per), :, p * half:(p + 1) * half] = y.reshape(per, rows, half)
            return carry

        lax.fori_loop(0, blocks, step, 0, unroll=4)

    def unpack(p, a, e):
        def step(b, carry):
            x = recv[a, pl.ds(b * per, per), :, p * half:(p + 1) * half].reshape(256, half)
            y = nn(pt_s[...], x).reshape(ROWS, BLOCK, half)
            in_s[e, p * ROWS:(p + 1) * ROWS, pl.ds(b * BLOCK, BLOCK), :] = y
            return carry

        lax.fori_loop(0, blocks, step, 0, unroll=4)

    def channel_pair(a, at):
        x = recv[a, :, at:at + 16, :].astype(F32).reshape(n, 2, ROWS, width)
        return [x[:, h].reshape(width, width).astype(BF16) for h in range(2)]

    def put_pair(a, at, items):
        x = jnp.concatenate([item.reshape(n, ROWS, width) for item in items], axis=1)
        send[a, :, at:at + 16, :] = x.astype(BF16)

    def triangle(t, la, ra, pa):
        for cc in range(2):
            channels_here(cc, (la, ra))
            for cp in range(cc * group // 4, (cc + 1) * group // 4):
                left, right = channel_pair(la, cp * 16), channel_pair(ra, cp * 16)
                items = []
                for h in range(2):
                    mats_s[t, 0, 2 * cp + h] = left[h]
                    mats_s[t, 1, 2 * cp + h] = right[h]
                    items.append(nt(left[h], right[h]) if t == 0 else tn(left[h], right[h]))
                put_pair(pa, cp * 16, items)
            to_pairs(cc, (pa,))

    def triangle_back(t, da, la, ra):
        for cc in range(2):
            channels_here(cc, (da,))
            for cp in range(cc * group // 4, (cc + 1) * group // 4):
                grads = channel_pair(da, cp * 16)
                dl, dr = [], []
                for h in range(2):
                    left, right = mats_s[t, 0, 2 * cp + h], mats_s[t, 1, 2 * cp + h]
                    if t == 0:
                        dl.append(nn(grads[h], right))
                        dr.append(tn(grads[h], left))
                    else:
                        dl.append(nt(right, grads[h]))
                        dr.append(nn(left, grads[h]))
                put_pair(la, cp * 16, dl)
                put_pair(ra, cp * 16, dr)
            to_pairs(cc, (la, ra))

    def front(t, q, z):
        normed, inv = norm(z.astype(F32))
        nb = normed.astype(BF16)
        nrm_s[t, q], istd_s[t, q], nb_s[t, q] = normed, inv, nb
        make_edge(t, 0, q, nb)

    def make_edge(t, e, q, nb):
        value = nn(pwt_s[t, 2 * e * CH:(2 * e + 1) * CH, :], nb)
        scale = pm_s[pl.ds(q, 1), :] * sigmoid(nn(pwt_s[t, (2 * e + 1) * CH:(2 * e + 2) * CH, :], nb))
        edge = scale * value
        side_s[t, 2 * e, q] = scale
        side_s[t, 2 * e + 1, q] = edge
        edge_s[e, q] = edge.astype(BF16)

    def gates(t):
        def step(q, carry):
            gate_s[t, q] = sigmoid(nn(pwt_s[t, 4 * CH:5 * CH, :], nb_s[t, q]))
            return carry

        lax.fori_loop(0, 2 * ROWS, step, 0, unroll=8)

    def rear(t, q):
        normed, inv = norm(in_s[0, q])
        nb = normed.astype(BF16)
        update = nn(owt_s[t], nb)
        pn_s[t, q], pstd_s[t, q], pnb_s[t, q], upd_s[t, q] = normed, inv, nb, update
        return (z_s[t, q].astype(F32) + gate_s[t, q] * update).astype(BF16)

    def rear_back(t, q, up):
        gate = gate_s[t, q]
        dupd = (up * gate).astype(BF16)
        dupd_s[t, q] = dupd
        dproj_s[t, 4, q] = (up * upd_s[t, q] * gate * (1.0 - gate)).astype(BF16)
        g = nn(ow_ref[t], dupd)
        edge_s[0, q] = norm_back(pn_s[t, q], pstd_s[t, q], g).astype(BF16)

    def edge_back(t, q):
        for e in range(2):
            grad, scale = in_s[e, q], side_s[t, 2 * e, q]
            dproj_s[t, 2 * e, q] = (grad * scale).astype(BF16)
            dproj_s[t, 2 * e + 1, q] = (grad * side_s[t, 2 * e + 1, q] * (1.0 - scale)).astype(BF16)

    def front_back(t, q, up):
        h = nn(pw_ref[t, :, 0:CH], dproj_s[t, 0, q])
        for b in range(1, 5):
            h += nn(pw_ref[t, :, b * CH:(b + 1) * CH], dproj_s[t, b, q])
        return (up + norm_back(nrm_s[t, q], istd_s[t, q], h)).astype(BF16)

    early_rows, late_rows = 8 * CH // n, 4 * CH // n

    def out_grad(t):
        total = nt(pnb_s[t, 0], dupd_s[t, 0])
        for q in range(1, 2 * ROWS):
            total += nt(pnb_s[t, q], dupd_s[t, q])
        return total

    def proj_grad(t, b, p=None):
        first, last = (0, 2 * ROWS) if p is None else (p * ROWS, (p + 1) * ROWS)
        total = nt(nb_s[t, first], dproj_s[t, b, first])
        for q in range(first + 1, last):
            total += nt(nb_s[t, q], dproj_s[t, b, q])
        return total

    def piece(at, size):
        return pl.ds(pl.multiple_of(at * size, size), size)

    def scatter(g, r, size, k):
        r[me] = g[piece(me, size), :]

        def go(to):
            pltpu.make_async_remote_copy(
                src_ref=g.at[piece(to, size)], dst_ref=r.at[me],
                send_sem=gsend_sem.at[k], recv_sem=grecv_sem.at[k],
                device_id={"dap": to}, device_id_type=MESH,
            ).start()

        to_all(go)

    def spread(x, r, k):
        def go(to):
            pltpu.make_async_remote_copy(
                src_ref=x, dst_ref=r.at[me], send_sem=gsend_sem.at[k], recv_sem=grecv_sem.at[k],
                device_id={"dap": to}, device_id_type=MESH,
            ).start()

        to_all(go)

    def across(x, y, k):
        y[mine] = x[...]
        for t in range(1, dp):
            pltpu.make_async_remote_copy(
                src_ref=x, dst_ref=y.at[mine], send_sem=gsend_sem.at[k], recv_sem=grecv_sem.at[k],
                device_id={"dp": lax.rem(mine + t, dp)}, device_id_type=MESH,
            ).start()

    def bulk(r, count, k):
        return pltpu.make_async_remote_copy(
            src_ref=r.at[pl.ds(0, count)], dst_ref=r.at[pl.ds(0, count)],
            send_sem=gsend_sem.at[k], recv_sem=grecv_sem.at[k],
            device_id={"dap": lax.rem(me + 1, n)}, device_id_type=MESH,
        )

    def summed(r, count):
        total = r[0].astype(F32)
        for t in range(1, count):
            total += r[t].astype(F32)
        return total

    inverse = 1.0 / (dp * width)

    def loop(body, p):
        def step(i, carry):
            body(i, i + p * ROWS)
            return carry

        lax.fori_loop(0, ROWS, step, 0, unroll=8)

    for p in range(2):
        def begin(i, q):
            x = nt(eye_s[...], pair_ref[i, p * half:(p + 1) * half, :])
            z = (x + sc_s[pl.ds(q, 1), :] * bias_s[...]).astype(BF16)
            z_s[0, q] = z
            front(0, q, z)

        def begin_right(i, q):
            make_edge(0, 1, q, nb_s[0, q])

        loop(begin, p)
        pack(p, L1, 0)
        if p == 0:
            pl.semaphore_wait(barrier, n - 1 + dp - 1)
            to_channels(0, (L1,))
        loop(begin_right, p)
        pack(p, R1, 1)
        to_channels(p, (R1,) if p == 0 else (L1, R1))
    turn_weight(0, 4)
    for b in range(5):
        turn_weight(1, b)
    for t in range(2):
        owt_s[t] = nt(eye_s[...], ow_ref[t]).astype(BF16)
    pt_s[...] = one_hot(256, 256, lambda r, q: q == (r % BLOCK) * ROWS + r // BLOCK).astype(BF16)
    gates(0)
    for p in range(2):
        def turn(i, q):
            cot_s[q] = nt(eye_s[...], cot_ref[i, p * half:(p + 1) * half, :]).astype(BF16)

        loop(turn, p)
    triangle(0, L1, R1, P1)
    for p in range(2):
        def middle(i, q):
            z = rear(0, q)
            z_s[1, q] = z
            front(1, q, z)

        pairs_here(p, P1)
        unpack(p, P1, 0)
        def middle_right(i, q):
            make_edge(1, 1, q, nb_s[1, q])

        loop(middle, p)
        pack(p, L2, 0)
        if p == 0:
            to_channels(0, (L2,))
        loop(middle_right, p)
        pack(p, R2, 1)
        to_channels(p, (R2,) if p == 0 else (L2, R2))
    gates(1)
    triangle(1, L2, R2, P2)

    for p in range(2):
        def last(i, q):
            z_s[2, q] = rear(1, q)
            rear_back(1, q, cot_s[q].astype(F32))

        pairs_here(p, P2)
        unpack(p, P2, 0)
        loop(last, p)
        pack(p, DP2, 0)
        to_channels(p, (DP2,))
    for p in range(2):
        def write_out(i, q):
            outv_s[i, p * half:(p + 1) * half, :] = nt(eye_s[0:half, 0:half], z_s[2, q]).astype(BF16)

        loop(write_out, p)
    put_out = pltpu.make_async_copy(outv_s, out_ref, put_sem.at[0])
    put_out.start()
    ge_s[5 * CH:6 * CH, :] = out_grad(1).astype(BF16)
    triangle_back(1, DP2, DL2, DR2)
    ge_s[4 * CH:5 * CH, :] = proj_grad(1, 4).astype(BF16)

    for p in range(2):
        def back(i, q):
            edge_back(1, q)
            grad = front_back(1, q, cot_s[q].astype(F32))
            dz_s[0, q] = grad
            rear_back(0, q, grad.astype(F32))

        pairs_here(p, DL2)
        unpack(p, DL2, 0)
        pairs_here(p, DR2)
        unpack(p, DR2, 1)
        loop(back, p)
        pack(p, DP1, 0)
        to_channels(p, (DP1,))
    for b in range(4):
        ge_s[b * CH:(b + 1) * CH, :] = proj_grad(1, b).astype(BF16)
    ge_s[6 * CH:7 * CH, :] = proj_grad(0, 4).astype(BF16)
    ge_s[7 * CH:8 * CH, :] = out_grad(0).astype(BF16)
    scatter(ge_s, re_s, early_rows, 0)
    triangle_back(0, DP1, DL1, DR1)
    bulk(re_s, n - 1, 0).wait_recv()
    xe_s[...] = summed(re_s, n)
    across(xe_s, ye_s, 1)
    chain_s[...] = jnp.zeros_like(chain_s)
    for p in range(2):
        def end(i, q):
            edge_back(0, q)

        pairs_here(p, DL1)
        unpack(p, DL1, 0)
        pairs_here(p, DR1)
        unpack(p, DR1, 1)
        loop(end, p)
        for b in range(4):
            if p == 0:
                acc_s[b] = proj_grad(0, b, 0)
            else:
                gf_s[b * CH:(b + 1) * CH, :] = (acc_s[b] + proj_grad(0, b, 1)).astype(BF16)
        if p == 0:
            bulk(ye_s, dp - 1, 1).wait_recv()
            ae_s[me] = (summed(ye_s, dp) * inverse).astype(BF16)
            spread(ae_s.at[me], ae_s, 2)
    scatter(gf_s, rf_s, late_rows, 3)
    for p in range(2):
        def finish(i, q):
            grad = front_back(0, q, dz_s[0, q].astype(F32))
            dz_s[1, q] = grad
            chain_s[...] += grad.astype(F32) * sc_s[pl.ds(q, 1), :]

        loop(finish, p)
    column_sum = jnp.sum(chain_s[...], axis=1, keepdims=True)
    cg_s[...] = jnp.sum(diag * column_sum, axis=0, keepdims=True)
    cr_s[me] = cg_s[...]
    spread(cg_s, cr_s, 6)
    bulk(rf_s, n - 1, 3).wait_recv()
    xf_s[...] = summed(rf_s, n)
    across(xf_s, yf_s, 4)
    for p in range(2):
        def write_grad(i, q):
            pgv_s[i, p * half:(p + 1) * half, :] = nt(eye_s[0:half, 0:half], dz_s[1, q]).astype(BF16)

        loop(write_grad, p)
    put_grad = pltpu.make_async_copy(pgv_s, pg_ref, put_sem.at[1])
    put_grad.start()
    bulk(cr_s, n - 1, 6).wait_recv()
    cx_s[...] = summed(cr_s, n)
    across(cx_s, cy_s, 7)
    bulk(yf_s, dp - 1, 4).wait_recv()
    af_s[me] = (summed(yf_s, dp) * inverse).astype(BF16)
    spread(af_s.at[me], af_s, 5)
    bulk(ae_s, n - 1, 2).wait_recv()
    full = ae_s[...].reshape(8 * CH, CH).astype(F32)
    for b in range(5):
        gproj_ref[1, :, b * CH:(b + 1) * CH] = full[b * CH:(b + 1) * CH]
    gout_ref[1] = full[5 * CH:6 * CH]
    gproj_ref[0, :, 4 * CH:5 * CH] = full[6 * CH:7 * CH]
    gout_ref[0] = full[7 * CH:8 * CH]
    bulk(cy_s, dp - 1, 7).wait_recv()
    gchain_ref[...] = summed(cy_s, dp) * inverse

    def drain(a, carry):
        sent(a)
        return carry

    lax.fori_loop(0, 12, drain, 0)
    for r, count, k in ((re_s, n, 0), (ye_s, dp, 1), (ae_s, n, 2), (rf_s, n, 3), (yf_s, dp, 4), (cr_s, n, 6), (cy_s, dp, 7)):
        bulk(r, count - 1, k).wait_send()
    put_out.wait()
    put_grad.wait()
    bulk(af_s, n - 1, 5).wait_recv()
    full = af_s[...].reshape(4 * CH, CH).astype(F32)
    for b in range(4):
        gproj_ref[0, :, b * CH:(b + 1) * CH] = full[b * CH:(b + 1) * CH]
    bulk(af_s, n - 1, 5).wait_send()


def hand_over(*refs):
    count = (len(refs) - 2) // 3
    given, outs, held = refs[:count], refs[count:2 * count], refs[2 * count:3 * count]
    in_sem, out_sem = refs[-2:]
    fetched = [pltpu.make_async_copy(given[k], held[k], in_sem.at[k]) for k in range(count)]
    put = [pltpu.make_async_copy(held[k], outs[k], out_sem.at[k]) for k in range(count)]
    for copy in fetched:
        copy.start()
    for k in range(count):
        fetched[k].wait()
        put[k].start()
    for copy in put:
        copy.wait()


def body(n, dp, pair_in, residue_mask, chain_index, chain_bias, proj_weight, out_weight, cotangent):
    width = n * ROWS
    group = CH // n
    early_rows, late_rows = 8 * CH // n, 4 * CH // n
    tensor = (2 * ROWS, CH, width // 2)
    line = (2 * ROWS, 1, width // 2)
    vmem = pl.BlockSpec(memory_space=pltpu.VMEM)
    shapes = [
        jax.ShapeDtypeStruct((ROWS, width, CH), BF16),
        jax.ShapeDtypeStruct((ROWS, width, CH), BF16),
        jax.ShapeDtypeStruct((2, CH, 5 * CH), F32),
        jax.ShapeDtypeStruct((2, CH, CH), F32),
        jax.ShapeDtypeStruct((1, CH), F32),
    ]
    scratch = [
        pltpu.VMEM((CH, CH), BF16),
        pltpu.VMEM((256, 256), BF16),
        pltpu.VMEM((256, 256), BF16),
        pltpu.VMEM((2, 5 * CH, CH), BF16),
        pltpu.VMEM((2, CH, CH), BF16),
        pltpu.VMEM((CH, 1), F32),
        pltpu.VMEM((2 * ROWS, width // 2), F32),
        pltpu.VMEM((2 * ROWS, width // 2), F32),
        pltpu.VMEM((3,) + tensor, BF16),
        pltpu.VMEM(tensor, BF16),
        pltpu.VMEM((2,) + tensor, BF16),
        pltpu.VMEM((2,) + tensor, BF16),
        pltpu.VMEM((2,) + tensor, F32),
        pltpu.VMEM((2,) + line, F32),
        pltpu.VMEM((2, 4) + tensor, F32),
        pltpu.VMEM((2,) + tensor, F32),
        pltpu.VMEM((2,) + tensor, F32),
        pltpu.VMEM((2,) + tensor, BF16),
        pltpu.VMEM((2,) + line, F32),
        pltpu.VMEM((2,) + tensor, F32),
        pltpu.VMEM((2,) + tensor, BF16),
        pltpu.VMEM((2, 5) + tensor, BF16),
        pltpu.VMEM((2,) + tensor, BF16),
        pltpu.VMEM((2,) + tensor, F32),
        pltpu.VMEM((2, 2, group, width, width), BF16),
        pltpu.VMEM((CH, width // 2), F32),
        pltpu.VMEM((4, CH, CH), F32),
        pltpu.VMEM((12, n, group * ROWS, width), BF16),
        pltpu.VMEM((12, n, group * ROWS, width), BF16),
        pltpu.VMEM((8 * CH, CH), BF16),
        pltpu.VMEM((n, early_rows, CH), BF16),
        pltpu.VMEM((n, early_rows, CH), BF16),
        pltpu.VMEM((4 * CH, CH), BF16),
        pltpu.VMEM((n, late_rows, CH), BF16),
        pltpu.VMEM((n, late_rows, CH), BF16),
        pltpu.VMEM((early_rows, CH), F32),
        pltpu.VMEM((dp, early_rows, CH), F32),
        pltpu.VMEM((late_rows, CH), F32),
        pltpu.VMEM((dp, late_rows, CH), F32),
        pltpu.VMEM((1, CH), F32),
        pltpu.VMEM((n, 1, CH), F32),
        pltpu.VMEM((1, CH), F32),
        pltpu.VMEM((dp, 1, CH), F32),
        pltpu.VMEM((ROWS, width, CH), BF16),
        pltpu.VMEM((ROWS, width, CH), BF16),
        pltpu.SemaphoreType.DMA((12,)),
        pltpu.SemaphoreType.DMA((12, 3)),
        pltpu.SemaphoreType.DMA((8,)),
        pltpu.SemaphoreType.DMA((8,)),
        pltpu.SemaphoreType.DMA((2,)),
    ]
    results = pl.pallas_call(
        functools.partial(kernel, n, dp),
        out_shape=shapes,
        in_specs=[vmem] * 7,
        out_specs=[pl.BlockSpec(memory_space=pl.ANY)] * 2 + [vmem] * 3,
        scratch_shapes=scratch,
        compiler_params=pltpu.CompilerParams(
            collective_id=0, has_side_effects=True, vmem_limit_bytes=62 * 1024 * 1024
        ),
    )(
        pair_in[0], residue_mask, chain_index, chain_bias.reshape(1, CH),
        proj_weight, out_weight, cotangent[0],
    )
    anywhere = pl.BlockSpec(memory_space=pl.ANY)
    out_pair, pair_grad, grad_proj, grad_out, grad_chain = pl.pallas_call(
        hand_over,
        out_shape=shapes,
        in_specs=[anywhere] * 5,
        out_specs=[anywhere] * 5,
        scratch_shapes=[pltpu.VMEM(shape.shape, shape.dtype) for shape in shapes]
        + [pltpu.SemaphoreType.DMA((5,)), pltpu.SemaphoreType.DMA((5,))],
        compiler_params=pltpu.CompilerParams(vmem_limit_bytes=62 * 1024 * 1024),
    )(*results)
    return out_pair[None], pair_grad[None], grad_proj, grad_out, grad_chain.reshape(CH)


def solution(mesh):
    n, dp = mesh.shape["dap"], mesh.shape["dp"]
    rows = P("dp", "dap", None, None)
    return jax.shard_map(
        functools.partial(body, n, dp),
        mesh=mesh,
        in_specs=(rows, P("dp", None), P("dp", None), P(), P(), P(), rows),
        out_specs=(rows, rows, P(), P(), P()),
        check_vma=False,
    )
```

```python
import functools

import jax
import jax.numpy as jnp
from jax import lax
from jax.experimental import pallas as pl
from jax.experimental.pallas import tpu as pltpu
from jax.sharding import PartitionSpec as P

EPSILON = 1e-05
MESH = pl.DeviceIdType.MESH
F32 = jnp.float32
BF16 = jnp.bfloat16
ROWS = 8
CH = 128
BLOCK = 32

L1, R1, P1, L2, R2, P2, DP2, DL2, DR2, DP1, DL1, DR1 = range(12)


def nt(a, b):
    return lax.dot_general(a, b, (((1,), (1,)), ((), ())), preferred_element_type=F32)


def tn(a, b):
    return lax.dot_general(a, b, (((0,), (0,)), ((), ())), preferred_element_type=F32)


def nn(a, b):
    return jnp.dot(a, b, preferred_element_type=F32)


def one_hot(rows, columns, wanted):
    r = lax.broadcasted_iota(jnp.int32, (rows, columns), 0)
    q = lax.broadcasted_iota(jnp.int32, (rows, columns), 1)
    return jnp.where(wanted(r, q), 1.0, 0.0).astype(F32)


def sigmoid(x):
    return 0.5 * jnp.tanh(0.5 * x) + 0.5


def norm(x):
    centred = x - jnp.mean(x, axis=0, keepdims=True)
    inv = lax.rsqrt(jnp.mean(centred * centred, axis=0, keepdims=True) + EPSILON)
    return centred * inv, inv


def norm_back(normed, inv, g):
    first = jnp.mean(g, axis=0, keepdims=True)
    second = jnp.mean(g * normed, axis=0, keepdims=True)
    return (g - first - normed * second) * inv


def kernel(
    n, dp, pair_ref, mask_ref, chain_ref, bias_ref, pw_ref, ow_ref, cot_ref,
    out_ref, pg_ref, gproj_ref, gout_ref, gchain_ref,
    eye_s, pf_s, pt_s, pwt_s, owt_s, bias_s, pm_s, sc_s,
    z_s, cot_s, dz_s, nb_s, nrm_s, istd_s, side_s, gate_s, pn_s, pnb_s, pstd_s, upd_s,
    dupd_s, dproj_s, edge_s, in_s, mats_s, chain_s, acc_s,
    send, recv, ge_s, re_s, ae_s, gf_s, rf_s, af_s, xe_s, ye_s, xf_s, yf_s, cg_s, cr_s, cx_s, cy_s, outv_s, pgv_s,
    send_sem, recv_sem, gsend_sem, grecv_sem, put_sem,
):
    width = n * ROWS
    half = width // 2
    group = CH // n
    rows = group * ROWS
    half_rows = rows // 2
    per = BLOCK * ROWS // rows
    blocks = CH // BLOCK
    me = lax.axis_index("dap")
    mine = lax.axis_index("dp")

    barrier = pltpu.get_barrier_semaphore()

    def greet(t, carry):
        pl.semaphore_signal(barrier, inc=1, device_id={"dap": lax.rem(me + t, n)}, device_id_type=MESH)
        return carry

    lax.fori_loop(1, n, greet, 0)

    def greet_dp(t, carry):
        pl.semaphore_signal(barrier, inc=1, device_id={"dp": lax.rem(mine + t, dp)}, device_id_type=MESH)
        return carry

    lax.fori_loop(1, dp, greet_dp, 0)

    eye_s[...] = one_hot(CH, CH, lambda r, q: r == q).astype(BF16)
    pf_s[...] = one_hot(256, 256, lambda r, q: q == (r % ROWS) * BLOCK + r // ROWS).astype(BF16)
    diag = one_hot(CH, CH, lambda r, q: r == q)
    bias_s[...] = jnp.sum(diag * bias_ref[...], axis=1, keepdims=True)

    def turn_weight(t, b):
        pwt_s[t, b * CH:(b + 1) * CH, :] = nt(eye_s[...], pw_ref[t, :, b * CH:(b + 1) * CH]).astype(BF16)

    for b in range(4):
        turn_weight(0, b)
    live = mask_ref[...].astype(F32)
    chain = chain_ref[...].astype(F32)
    own = one_hot(ROWS, width, lambda r, q: q == r + ROWS * me)
    pair_mask = jnp.sum(own * live, axis=1, keepdims=True) * live
    same = jnp.where(jnp.sum(own * chain, axis=1, keepdims=True) == chain, 1.0, 0.0)
    for p in range(2):
        pm_s[p * ROWS:(p + 1) * ROWS, :] = pair_mask[:, p * half:(p + 1) * half]
        sc_s[p * ROWS:(p + 1) * ROWS, :] = same[:, p * half:(p + 1) * half]

    if n == 32:
        row, plane, column = me // 8, (me // 4) % 2, me % 4
        planes = [4 * lax.rem(plane + k, 2) for k in range(2)]
        columns = [lax.rem(column + k, 4) for k in range(4)]

    def to_all(start):
        if n != 32:
            lax.fori_loop(1, n, lambda t, carry: (start(lax.rem(me + t, n)), carry)[1], 0)
            return

        lines = [8 * lax.rem(row + k, 4) for k in range(4)]
        away = (0, 1, 2, 1)
        order = [(k, h, c) for k in range(4) for h in range(2) for c in range(4)]
        order.sort(key=lambda d: (-(away[d[0]] + d[1] + away[d[2]]), (d[0] + 2 * d[2] + d[1]) % 4))
        for k, h, c in order[:-1]:
            start(lines[k] + planes[h] + columns[c])

    def push(messages):
        for a, r0, rn, p, k in messages:
            at = (a, pl.ds(me, 1), slice(r0, r0 + rn), slice(p * half, (p + 1) * half))
            recv[at] = send[at]

        def go(to):
            for a, r0, rn, p, k in messages:
                part = (pl.ds(r0, rn), pl.ds(p * half, half))
                pltpu.make_async_remote_copy(
                    src_ref=send.at[(a, to) + part], dst_ref=recv.at[(a, me) + part],
                    send_sem=send_sem.at[a], recv_sem=recv_sem.at[a, k],
                    device_id={"dap": to}, device_id_type=MESH,
                ).start()

        to_all(go)

    def arrived(a, r0, rn, p, k):
        part = (a, pl.ds(0, n - 1), pl.ds(r0, rn), pl.ds(p * half, half))
        pltpu.make_async_remote_copy(
            src_ref=send.at[part], dst_ref=recv.at[part],
            send_sem=send_sem.at[a], recv_sem=recv_sem.at[a, k],
            device_id={"dap": lax.rem(me + 1, n)}, device_id_type=MESH,
        ).wait_recv()

    def sent(a):
        part = (a, pl.ds(0, n - 1))
        pltpu.make_async_remote_copy(
            src_ref=send.at[part], dst_ref=recv.at[part],
            send_sem=send_sem.at[a], recv_sem=recv_sem.at[a, 0],
            device_id={"dap": lax.rem(me + 1, n)}, device_id_type=MESH,
        ).wait_send()

    def to_channels(p, items):
        if p == 0:
            push([(a, 0, rows, 0, 0) for a in items])
        else:
            push([(a, 0, half_rows, 1, 1) for a in items])
            push([(a, half_rows, half_rows, 1, 2) for a in items])

    def channels_here(cc, items):
        for a in items:
            if cc == 0:
                arrived(a, 0, rows, 0, 0)
            arrived(a, cc * half_rows, half_rows, 1, 1 + cc)

    def to_pairs(cc, items):
        push([(a, cc * half_rows, half_rows, 0, 0) for a in items])
        if cc == 1:
            for a in items:
                push([(a, 0, rows, 1, 1)])

    def pairs_here(p, a):
        arrived(a, 0, rows, p, p)

    def pack(p, a, e):
        def step(b, carry):
            x = edge_s[e, p * ROWS:(p + 1) * ROWS, pl.ds(b * BLOCK, BLOCK), :].reshape(256, half)
            y = nn(pf_s[...], x).astype(BF16)
            send[a, pl.ds(b * per, per), :, p * half:(p + 1) * half] = y.reshape(per, rows, half)
            return carry

        lax.fori_loop(0, blocks, step, 0, unroll=4)

    def unpack(p, a, e):
        def step(b, carry):
            x = recv[a, pl.ds(b * per, per), :, p * half:(p + 1) * half].reshape(256, half)
            y = nn(pt_s[...], x).reshape(ROWS, BLOCK, half)
            in_s[e, p * ROWS:(p + 1) * ROWS, pl.ds(b * BLOCK, BLOCK), :] = y
            return carry

        lax.fori_loop(0, blocks, step, 0, unroll=4)

    def channel_pair(a, at):
        x = recv[a, :, at:at + 16, :].astype(F32).reshape(n, 2, ROWS, width)
        return [x[:, h].reshape(width, width).astype(BF16) for h in range(2)]

    def put_pair(a, at, items):
        x = jnp.concatenate([item.reshape(n, ROWS, width) for item in items], axis=1)
        send[a, :, at:at + 16, :] = x.astype(BF16)

    def triangle(t, la, ra, pa):
        for cc in range(2):
            channels_here(cc, (la, ra))
            for cp in range(cc * group // 4, (cc + 1) * group // 4):
                left, right = channel_pair(la, cp * 16), channel_pair(ra, cp * 16)
                items = []
                for h in range(2):
                    mats_s[t, 0, 2 * cp + h] = left[h]
                    mats_s[t, 1, 2 * cp + h] = right[h]
                    items.append(nt(left[h], right[h]) if t == 0 else tn(left[h], right[h]))
                put_pair(pa, cp * 16, items)
            to_pairs(cc, (pa,))

    def triangle_back(t, da, la, ra):
        for cc in range(2):
            channels_here(cc, (da,))
            for cp in range(cc * group // 4, (cc + 1) * group // 4):
                grads = channel_pair(da, cp * 16)
                dl, dr = [], []
                for h in range(2):
                    left, right = mats_s[t, 0, 2 * cp + h], mats_s[t, 1, 2 * cp + h]
                    if t == 0:
                        dl.append(nn(grads[h], right))
                        dr.append(tn(grads[h], left))
                    else:
                        dl.append(nt(right, grads[h]))
                        dr.append(nn(left, grads[h]))
                put_pair(la, cp * 16, dl)
                put_pair(ra, cp * 16, dr)
            to_pairs(cc, (la, ra))

    def front(t, q, z):
        normed, inv = norm(z.astype(F32))
        nb = normed.astype(BF16)
        nrm_s[t, q], istd_s[t, q], nb_s[t, q] = normed, inv, nb
        make_edge(t, 0, q, nb)

    def make_edge(t, e, q, nb):
        both = nn(pwt_s[t, 2 * e * CH:(2 * e + 2) * CH, :], nb)
        scale = pm_s[pl.ds(q, 1), :] * sigmoid(both[CH:])
        edge = scale * both[:CH]
        side_s[t, 2 * e, q] = scale
        side_s[t, 2 * e + 1, q] = edge
        edge_s[e, q] = edge.astype(BF16)

    def gates(t):
        def step(q, carry):
            gate_s[t, q] = sigmoid(nn(pwt_s[t, 4 * CH:5 * CH, :], nb_s[t, q]))
            return carry

        lax.fori_loop(0, 2 * ROWS, step, 0, unroll=8)

    def rear(t, q):
        normed, inv = norm(in_s[0, q])
        nb = normed.astype(BF16)
        update = nn(owt_s[t], nb)
        pn_s[t, q], pstd_s[t, q], pnb_s[t, q], upd_s[t, q] = normed, inv, nb, update
        return (z_s[t, q].astype(F32) + gate_s[t, q] * update).astype(BF16)

    def rear_back(t, q, up):
        gate = gate_s[t, q]
        dupd = (up * gate).astype(BF16)
        dupd_s[t, q] = dupd
        g = nn(ow_ref[t], dupd)
        edge_s[0, q] = norm_back(pn_s[t, q], pstd_s[t, q], g).astype(BF16)

    def gate_back(t, q, up):
        gate = gate_s[t, q]
        dproj_s[t, q, 4 * CH:5 * CH, :] = (up * upd_s[t, q] * gate * (1.0 - gate)).astype(BF16)

    def edge_back(t, e, q):
        grad, scale = in_s[e, q], side_s[t, 2 * e, q]
        dproj_s[t, q, 2 * e * CH:(2 * e + 1) * CH, :] = (grad * scale).astype(BF16)
        dproj_s[t, q, (2 * e + 1) * CH:(2 * e + 2) * CH, :] = (
            grad * side_s[t, 2 * e + 1, q] * (1.0 - scale)
        ).astype(BF16)

    def front_back(t, q, up):
        h = nn(pw_ref[t], dproj_s[t, q])
        return (up + norm_back(nrm_s[t, q], istd_s[t, q], h)).astype(BF16)

    early_rows, late_rows = 8 * CH // n, 4 * CH // n

    def out_grad(t):
        total = nt(pnb_s[t, 0], dupd_s[t, 0])
        for q in range(1, 2 * ROWS):
            total += nt(pnb_s[t, q], dupd_s[t, q])
        return total

    def proj_grad(t, b, p=None):
        first, last = (0, 2 * ROWS) if p is None else (p * ROWS, (p + 1) * ROWS)
        total = nt(nb_s[t, first], dproj_s[t, first, b * CH:(b + 1) * CH, :])
        for q in range(first + 1, last):
            total += nt(nb_s[t, q], dproj_s[t, q, b * CH:(b + 1) * CH, :])
        return total

    def piece(at, size):
        return pl.ds(pl.multiple_of(at * size, size), size)

    def scatter(g, r, size, k):
        r[me] = g[piece(me, size), :]

        def go(to):
            pltpu.make_async_remote_copy(
                src_ref=g.at[piece(to, size)], dst_ref=r.at[me],
                send_sem=gsend_sem.at[k], recv_sem=grecv_sem.at[k],
                device_id={"dap": to}, device_id_type=MESH,
            ).start()

        to_all(go)

    def spread(x, r, k):
        def go(to):
            pltpu.make_async_remote_copy(
                src_ref=x, dst_ref=r.at[me], send_sem=gsend_sem.at[k], recv_sem=grecv_sem.at[k],
                device_id={"dap": to}, device_id_type=MESH,
            ).start()

        to_all(go)

    def across(x, y, k):
        y[mine] = x[...]
        for t in range(1, dp):
            pltpu.make_async_remote_copy(
                src_ref=x, dst_ref=y.at[mine], send_sem=gsend_sem.at[k], recv_sem=grecv_sem.at[k],
                device_id={"dp": lax.rem(mine + t, dp)}, device_id_type=MESH,
            ).start()

    def bulk(r, count, k):
        return pltpu.make_async_remote_copy(
            src_ref=r.at[pl.ds(0, count)], dst_ref=r.at[pl.ds(0, count)],
            send_sem=gsend_sem.at[k], recv_sem=grecv_sem.at[k],
            device_id={"dap": lax.rem(me + 1, n)}, device_id_type=MESH,
        )

    def summed(r, count):
        total = r[0].astype(F32)
        for t in range(1, count):
            total += r[t].astype(F32)
        return total

    inverse = 1.0 / (dp * width)

    def loop(body, p):
        def step(i, carry):
            body(i, i + p * ROWS)
            return carry

        lax.fori_loop(0, ROWS, step, 0, unroll=8)

    for p in range(2):
        def begin(i, q):
            x = nt(eye_s[...], pair_ref[i, p * half:(p + 1) * half, :])
            z = (x + sc_s[pl.ds(q, 1), :] * bias_s[...]).astype(BF16)
            z_s[0, q] = z
            front(0, q, z)

        def begin_right(i, q):
            make_edge(0, 1, q, nb_s[0, q])

        loop(begin, p)
        pack(p, L1, 0)
        if p == 0:
            pl.semaphore_wait(barrier, n - 1 + dp - 1)
            to_channels(0, (L1,))
        loop(begin_right, p)
        pack(p, R1, 1)
        to_channels(p, (R1,) if p == 0 else (L1, R1))
    turn_weight(0, 4)
    for b in range(5):
        turn_weight(1, b)
    for t in range(2):
        owt_s[t] = nt(eye_s[...], ow_ref[t]).astype(BF16)
    pt_s[...] = one_hot(256, 256, lambda r, q: q == (r % BLOCK) * ROWS + r // BLOCK).astype(BF16)
    gates(0)
    for p in range(2):
        def turn(i, q):
            cot_s[q] = nt(eye_s[...], cot_ref[i, p * half:(p + 1) * half, :]).astype(BF16)

        loop(turn, p)
    triangle(0, L1, R1, P1)
    for p in range(2):
        def middle(i, q):
            z = rear(0, q)
            z_s[1, q] = z
            front(1, q, z)

        pairs_here(p, P1)
        unpack(p, P1, 0)
        def middle_right(i, q):
            make_edge(1, 1, q, nb_s[1, q])

        loop(middle, p)
        pack(p, L2, 0)
        if p == 0:
            to_channels(0, (L2,))
        loop(middle_right, p)
        pack(p, R2, 1)
        to_channels(p, (R2,) if p == 0 else (L2, R2))
    gates(1)
    triangle(1, L2, R2, P2)

    for p in range(2):
        def last(i, q):
            z_s[2, q] = rear(1, q)
            rear_back(1, q, cot_s[q].astype(F32))

        pairs_here(p, P2)
        unpack(p, P2, 0)
        loop(last, p)
        pack(p, DP2, 0)
        to_channels(p, (DP2,))
    for p in range(2):
        def write_out(i, q):
            outv_s[i, p * half:(p + 1) * half, :] = nt(eye_s[0:half, 0:half], z_s[2, q]).astype(BF16)

        def gate_two(i, q):
            gate_back(1, q, cot_s[q].astype(F32))

        loop(write_out, p)
        loop(gate_two, p)
    put_out = pltpu.make_async_copy(outv_s, out_ref, put_sem.at[0])
    put_out.start()
    ge_s[5 * CH:6 * CH, :] = out_grad(1).astype(BF16)
    triangle_back(1, DP2, DL2, DR2)
    ge_s[4 * CH:5 * CH, :] = proj_grad(1, 4).astype(BF16)

    for p in range(2):
        def back(i, q):
            edge_back(1, 1, q)
            grad = front_back(1, q, cot_s[q].astype(F32))
            dz_s[0, q] = grad
            rear_back(0, q, grad.astype(F32))

        def back_left(i, q):
            edge_back(1, 0, q)

        pairs_here(p, DL2)
        unpack(p, DL2, 0)
        loop(back_left, p)
        pairs_here(p, DR2)
        unpack(p, DR2, 1)
        loop(back, p)
        pack(p, DP1, 0)
        to_channels(p, (DP1,))
    for b in range(4):
        ge_s[b * CH:(b + 1) * CH, :] = proj_grad(1, b).astype(BF16)
    for p in range(2):
        def gate_one(i, q):
            gate_back(0, q, dz_s[0, q].astype(F32))

        loop(gate_one, p)
    ge_s[6 * CH:7 * CH, :] = proj_grad(0, 4).astype(BF16)
    ge_s[7 * CH:8 * CH, :] = out_grad(0).astype(BF16)
    scatter(ge_s, re_s, early_rows, 0)
    triangle_back(0, DP1, DL1, DR1)
    bulk(re_s, n - 1, 0).wait_recv()
    xe_s[...] = summed(re_s, n)
    across(xe_s, ye_s, 1)
    chain_s[...] = jnp.zeros_like(chain_s)
    for p in range(2):
        for e in range(2):
            def end(i, q):
                edge_back(0, e, q)

            pairs_here(p, (DL1, DR1)[e])
            unpack(p, (DL1, DR1)[e], e)
            loop(end, p)
            for b in (2 * e, 2 * e + 1):
                if p == 0:
                    acc_s[b] = proj_grad(0, b, 0)
                else:
                    gf_s[b * CH:(b + 1) * CH, :] = (acc_s[b] + proj_grad(0, b, 1)).astype(BF16)
        if p == 0:
            bulk(ye_s, dp - 1, 1).wait_recv()
            ae_s[me] = (summed(ye_s, dp) * inverse).astype(BF16)
            spread(ae_s.at[me], ae_s, 2)
    scatter(gf_s, rf_s, late_rows, 3)
    for p in range(2):
        def finish(i, q):
            grad = front_back(0, q, dz_s[0, q].astype(F32))
            dz_s[1, q] = grad
            chain_s[...] += grad.astype(F32) * sc_s[pl.ds(q, 1), :]

        loop(finish, p)
    column_sum = jnp.sum(chain_s[...], axis=1, keepdims=True)
    cg_s[...] = jnp.sum(diag * column_sum, axis=0, keepdims=True)
    cr_s[me] = cg_s[...]
    spread(cg_s, cr_s, 6)
    bulk(rf_s, n - 1, 3).wait_recv()
    xf_s[...] = summed(rf_s, n)
    across(xf_s, yf_s, 4)
    for p in range(2):
        def write_grad(i, q):
            pgv_s[i, p * half:(p + 1) * half, :] = nt(eye_s[0:half, 0:half], dz_s[1, q]).astype(BF16)

        loop(write_grad, p)
    put_grad = pltpu.make_async_copy(pgv_s, pg_ref, put_sem.at[1])
    put_grad.start()
    bulk(cr_s, n - 1, 6).wait_recv()
    cx_s[...] = summed(cr_s, n)
    across(cx_s, cy_s, 7)
    bulk(yf_s, dp - 1, 4).wait_recv()
    af_s[me] = (summed(yf_s, dp) * inverse).astype(BF16)
    spread(af_s.at[me], af_s, 5)
    bulk(ae_s, n - 1, 2).wait_recv()
    full = ae_s[...].reshape(8 * CH, CH).astype(F32)
    for b in range(5):
        gproj_ref[1, :, b * CH:(b + 1) * CH] = full[b * CH:(b + 1) * CH]
    gout_ref[1] = full[5 * CH:6 * CH]
    gproj_ref[0, :, 4 * CH:5 * CH] = full[6 * CH:7 * CH]
    gout_ref[0] = full[7 * CH:8 * CH]
    bulk(cy_s, dp - 1, 7).wait_recv()
    gchain_ref[...] = summed(cy_s, dp) * inverse

    def drain(a, carry):
        sent(a)
        return carry

    lax.fori_loop(0, 12, drain, 0)
    for r, count, k in ((re_s, n, 0), (ye_s, dp, 1), (ae_s, n, 2), (rf_s, n, 3), (yf_s, dp, 4), (cr_s, n, 6), (cy_s, dp, 7)):
        bulk(r, count - 1, k).wait_send()
    put_out.wait()
    put_grad.wait()
    bulk(af_s, n - 1, 5).wait_recv()
    full = af_s[...].reshape(4 * CH, CH).astype(F32)
    for b in range(4):
        gproj_ref[0, :, b * CH:(b + 1) * CH] = full[b * CH:(b + 1) * CH]
    bulk(af_s, n - 1, 5).wait_send()


def hand_over(*refs):
    count = (len(refs) - 2) // 3
    given, outs, held = refs[:count], refs[count:2 * count], refs[2 * count:3 * count]
    in_sem, out_sem = refs[-2:]
    fetched = [pltpu.make_async_copy(given[k], held[k], in_sem.at[k]) for k in range(count)]
    put = [pltpu.make_async_copy(held[k], outs[k], out_sem.at[k]) for k in range(count)]
    for copy in fetched:
        copy.start()
    for k in range(count):
        fetched[k].wait()
        put[k].start()
    for copy in put:
        copy.wait()


def body(n, dp, pair_in, residue_mask, chain_index, chain_bias, proj_weight, out_weight, cotangent):
    width = n * ROWS
    group = CH // n
    early_rows, late_rows = 8 * CH // n, 4 * CH // n
    tensor = (2 * ROWS, CH, width // 2)
    line = (2 * ROWS, 1, width // 2)
    vmem = pl.BlockSpec(memory_space=pltpu.VMEM)
    shapes = [
        jax.ShapeDtypeStruct((ROWS, width, CH), BF16),
        jax.ShapeDtypeStruct((ROWS, width, CH), BF16),
        jax.ShapeDtypeStruct((2, CH, 5 * CH), F32),
        jax.ShapeDtypeStruct((2, CH, CH), F32),
        jax.ShapeDtypeStruct((1, CH), F32),
    ]
    scratch = [
        pltpu.VMEM((CH, CH), BF16),
        pltpu.VMEM((256, 256), BF16),
        pltpu.VMEM((256, 256), BF16),
        pltpu.VMEM((2, 5 * CH, CH), BF16),
        pltpu.VMEM((2, CH, CH), BF16),
        pltpu.VMEM((CH, 1), F32),
        pltpu.VMEM((2 * ROWS, width // 2), F32),
        pltpu.VMEM((2 * ROWS, width // 2), F32),
        pltpu.VMEM((3,) + tensor, BF16),
        pltpu.VMEM(tensor, BF16),
        pltpu.VMEM((2,) + tensor, BF16),
        pltpu.VMEM((2,) + tensor, BF16),
        pltpu.VMEM((2,) + tensor, F32),
        pltpu.VMEM((2,) + line, F32),
        pltpu.VMEM((2, 4) + tensor, F32),
        pltpu.VMEM((2,) + tensor, F32),
        pltpu.VMEM((2,) + tensor, F32),
        pltpu.VMEM((2,) + tensor, BF16),
        pltpu.VMEM((2,) + line, F32),
        pltpu.VMEM((2,) + tensor, F32),
        pltpu.VMEM((2,) + tensor, BF16),
        pltpu.VMEM((2, 2 * ROWS, 5 * CH, width // 2), BF16),
        pltpu.VMEM((2,) + tensor, BF16),
        pltpu.VMEM((2,) + tensor, F32),
        pltpu.VMEM((2, 2, group, width, width), BF16),
        pltpu.VMEM((CH, width // 2), F32),
        pltpu.VMEM((4, CH, CH), F32),
        pltpu.VMEM((12, n, group * ROWS, width), BF16),
        pltpu.VMEM((12, n, group * ROWS, width), BF16),
        pltpu.VMEM((8 * CH, CH), BF16),
        pltpu.VMEM((n, early_rows, CH), BF16),
        pltpu.VMEM((n, early_rows, CH), BF16),
        pltpu.VMEM((4 * CH, CH), BF16),
        pltpu.VMEM((n, late_rows, CH), BF16),
        pltpu.VMEM((n, late_rows, CH), BF16),
        pltpu.VMEM((early_rows, CH), F32),
        pltpu.VMEM((dp, early_rows, CH), F32),
        pltpu.VMEM((late_rows, CH), F32),
        pltpu.VMEM((dp, late_rows, CH), F32),
        pltpu.VMEM((1, CH), F32),
        pltpu.VMEM((n, 1, CH), F32),
        pltpu.VMEM((1, CH), F32),
        pltpu.VMEM((dp, 1, CH), F32),
        pltpu.VMEM((ROWS, width, CH), BF16),
        pltpu.VMEM((ROWS, width, CH), BF16),
        pltpu.SemaphoreType.DMA((12,)),
        pltpu.SemaphoreType.DMA((12, 3)),
        pltpu.SemaphoreType.DMA((8,)),
        pltpu.SemaphoreType.DMA((8,)),
        pltpu.SemaphoreType.DMA((2,)),
    ]
    results = pl.pallas_call(
        functools.partial(kernel, n, dp),
        out_shape=shapes,
        in_specs=[vmem] * 7,
        out_specs=[pl.BlockSpec(memory_space=pl.ANY)] * 2 + [vmem] * 3,
        scratch_shapes=scratch,
        compiler_params=pltpu.CompilerParams(
            collective_id=0, has_side_effects=True, vmem_limit_bytes=62 * 1024 * 1024
        ),
    )(
        pair_in[0], residue_mask, chain_index, chain_bias.reshape(1, CH),
        proj_weight, out_weight, cotangent[0],
    )
    anywhere = pl.BlockSpec(memory_space=pl.ANY)
    out_pair, pair_grad, grad_proj, grad_out, grad_chain = pl.pallas_call(
        hand_over,
        out_shape=shapes,
        in_specs=[anywhere] * 5,
        out_specs=[anywhere] * 5,
        scratch_shapes=[pltpu.VMEM(shape.shape, shape.dtype) for shape in shapes]
        + [pltpu.SemaphoreType.DMA((5,)), pltpu.SemaphoreType.DMA((5,))],
        compiler_params=pltpu.CompilerParams(vmem_limit_bytes=62 * 1024 * 1024),
    )(*results)
    return out_pair[None], pair_grad[None], grad_proj, grad_out, grad_chain.reshape(CH)


def solution(mesh):
    n, dp = mesh.shape["dap"], mesh.shape["dp"]
    rows = P("dp", "dap", None, None)
    return jax.shard_map(
        functools.partial(body, n, dp),
        mesh=mesh,
        in_specs=(rows, P("dp", None), P("dp", None), P(), P(), P(), rows),
        out_specs=(rows, rows, P(), P(), P()),
        check_vma=False,
    )
```

```python
import functools

import jax
import jax.numpy as jnp
from jax import lax
from jax.experimental import pallas as pl
from jax.experimental.pallas import tpu as pltpu
from jax.sharding import PartitionSpec as P

EPSILON = 1e-05
MESH = pl.DeviceIdType.MESH
F32 = jnp.float32
BF16 = jnp.bfloat16
ROWS = 8
CH = 128
BLOCK = 32

L1, R1, P1, L2, R2, P2, DP2, DL2, DR2, DP1, DL1, DR1 = range(12)


def nt(a, b):
    return lax.dot_general(a, b, (((1,), (1,)), ((), ())), preferred_element_type=F32)


def tn(a, b):
    return lax.dot_general(a, b, (((0,), (0,)), ((), ())), preferred_element_type=F32)


def nn(a, b):
    return jnp.dot(a, b, preferred_element_type=F32)


def one_hot(rows, columns, wanted):
    r = lax.broadcasted_iota(jnp.int32, (rows, columns), 0)
    q = lax.broadcasted_iota(jnp.int32, (rows, columns), 1)
    return jnp.where(wanted(r, q), 1.0, 0.0).astype(F32)


def sigmoid(x):
    return 0.5 * jnp.tanh(0.5 * x) + 0.5


def norm(x):
    centred = x - jnp.mean(x, axis=0, keepdims=True)
    inv = lax.rsqrt(jnp.mean(centred * centred, axis=0, keepdims=True) + EPSILON)
    return centred * inv, inv


def norm_back(normed, inv, g):
    first = jnp.mean(g, axis=0, keepdims=True)
    second = jnp.mean(g * normed, axis=0, keepdims=True)
    return (g - first - normed * second) * inv


def kernel(
    n, dp, pair_in, mask_in, chain_in, bias_in, pw_in, ow_in, cot_in,
    out_ref, pg_ref, gproj_ref, gout_ref, gchain_ref,
    pair_ref, mask_ref, chain_ref, bias_ref, pw_ref, ow_ref, cot_ref, load_sem,
    eye_s, pf_s, pt_s, pwt_s, owt_s, bias_s, pm_s, sc_s,
    z_s, cot_s, dz_s, nb_s, nrm_s, istd_s, side_s, gate_s, pn_s, pnb_s, pstd_s, upd_s,
    dupd_s, dproj_s, edge_s, in_s, mats_s, chain_s, acc_s,
    send, recv, ge_s, re_s, ae_s, gf_s, rf_s, af_s, xe_s, ye_s, xf_s, yf_s, cg_s, cr_s, cx_s, cy_s, outv_s, pgv_s,
    send_sem, recv_sem, gsend_sem, grecv_sem, put_sem,
):
    width = n * ROWS
    half = width // 2
    group = CH // n
    rows = group * ROWS
    half_rows = rows // 2
    per = BLOCK * ROWS // rows
    blocks = CH // BLOCK
    me = lax.axis_index("dap")
    mine = lax.axis_index("dp")

    pairs = (
        (bias_in, bias_ref), (mask_in, mask_ref), (chain_in, chain_ref), (pw_in, pw_ref),
        (pair_in, pair_ref), (ow_in, ow_ref), (cot_in, cot_ref),
    )
    loads = [pltpu.make_async_copy(given, held, load_sem.at[k]) for k, (given, held) in enumerate(pairs)]
    for load in loads:
        load.start()
    barrier = pltpu.get_barrier_semaphore()

    def greet(t, carry):
        pl.semaphore_signal(barrier, inc=1, device_id={"dap": lax.rem(me + t, n)}, device_id_type=MESH)
        return carry

    lax.fori_loop(1, n, greet, 0)

    def greet_dp(t, carry):
        pl.semaphore_signal(barrier, inc=1, device_id={"dp": lax.rem(mine + t, dp)}, device_id_type=MESH)
        return carry

    lax.fori_loop(1, dp, greet_dp, 0)

    eye_s[...] = one_hot(CH, CH, lambda r, q: r == q).astype(BF16)
    pf_s[...] = one_hot(256, 256, lambda r, q: q == (r % ROWS) * BLOCK + r // ROWS).astype(BF16)
    diag = one_hot(CH, CH, lambda r, q: r == q)
    for load in loads[:4]:
        load.wait()
    bias_s[...] = jnp.sum(diag * bias_ref[...], axis=1, keepdims=True)

    def turn_weight(t, b):
        pwt_s[t, b * CH:(b + 1) * CH, :] = nt(eye_s[...], pw_ref[t, :, b * CH:(b + 1) * CH]).astype(BF16)

    for b in range(4):
        turn_weight(0, b)
    live = mask_ref[...].astype(F32)
    chain = chain_ref[...].astype(F32)
    own = one_hot(ROWS, width, lambda r, q: q == r + ROWS * me)
    pair_mask = jnp.sum(own * live, axis=1, keepdims=True) * live
    same = jnp.where(jnp.sum(own * chain, axis=1, keepdims=True) == chain, 1.0, 0.0)
    for p in range(2):
        pm_s[p * ROWS:(p + 1) * ROWS, :] = pair_mask[:, p * half:(p + 1) * half]
        sc_s[p * ROWS:(p + 1) * ROWS, :] = same[:, p * half:(p + 1) * half]

    if n == 32:
        row, plane, column = me // 8, (me // 4) % 2, me % 4
        planes = [4 * lax.rem(plane + k, 2) for k in range(2)]
        columns = [lax.rem(column + k, 4) for k in range(4)]

    def to_all(start):
        if n != 32:
            lax.fori_loop(1, n, lambda t, carry: (start(lax.rem(me + t, n)), carry)[1], 0)
            return

        lines = [8 * lax.rem(row + k, 4) for k in range(4)]
        away = (0, 1, 2, 1)
        order = [(k, h, c) for k in range(4) for h in range(2) for c in range(4)]
        order.sort(key=lambda d: (-(away[d[0]] + d[1] + away[d[2]]), (d[0] + 2 * d[2] + d[1]) % 4))
        for k, h, c in order[:-1]:
            start(lines[k] + planes[h] + columns[c])

    def push(messages):
        for a, r0, rn, p, k in messages:
            at = (a, pl.ds(me, 1), slice(r0, r0 + rn), slice(p * half, (p + 1) * half))
            recv[at] = send[at]

        def go(to):
            for a, r0, rn, p, k in messages:
                part = (pl.ds(r0, rn), pl.ds(p * half, half))
                pltpu.make_async_remote_copy(
                    src_ref=send.at[(a, to) + part], dst_ref=recv.at[(a, me) + part],
                    send_sem=send_sem.at[a], recv_sem=recv_sem.at[a, k],
                    device_id={"dap": to}, device_id_type=MESH,
                ).start()

        to_all(go)

    def arrived(a, r0, rn, p, k):
        part = (a, pl.ds(0, n - 1), pl.ds(r0, rn), pl.ds(p * half, half))
        pltpu.make_async_remote_copy(
            src_ref=send.at[part], dst_ref=recv.at[part],
            send_sem=send_sem.at[a], recv_sem=recv_sem.at[a, k],
            device_id={"dap": lax.rem(me + 1, n)}, device_id_type=MESH,
        ).wait_recv()

    def sent(a):
        part = (a, pl.ds(0, n - 1))
        pltpu.make_async_remote_copy(
            src_ref=send.at[part], dst_ref=recv.at[part],
            send_sem=send_sem.at[a], recv_sem=recv_sem.at[a, 0],
            device_id={"dap": lax.rem(me + 1, n)}, device_id_type=MESH,
        ).wait_send()

    def to_channels(p, items):
        if p == 0:
            push([(a, 0, rows, 0, 0) for a in items])
        else:
            push([(a, 0, half_rows, 1, 1) for a in items])
            push([(a, half_rows, half_rows, 1, 2) for a in items])

    def channels_here(cc, items):
        for a in items:
            if cc == 0:
                arrived(a, 0, rows, 0, 0)
            arrived(a, cc * half_rows, half_rows, 1, 1 + cc)

    def to_pairs(cc, items):
        push([(a, cc * half_rows, half_rows, 0, 0) for a in items])
        if cc == 1:
            for a in items:
                push([(a, 0, rows, 1, 1)])

    def pairs_here(p, a):
        arrived(a, 0, rows, p, p)

    def pack(p, a, e):
        def step(b, carry):
            x = edge_s[e, p * ROWS:(p + 1) * ROWS, pl.ds(b * BLOCK, BLOCK), :].reshape(256, half)
            y = nn(pf_s[...], x).astype(BF16)
            send[a, pl.ds(b * per, per), :, p * half:(p + 1) * half] = y.reshape(per, rows, half)
            return carry

        lax.fori_loop(0, blocks, step, 0, unroll=4)

    def unpack(p, a, e):
        def step(b, carry):
            x = recv[a, pl.ds(b * per, per), :, p * half:(p + 1) * half].reshape(256, half)
            y = nn(pt_s[...], x).reshape(ROWS, BLOCK, half)
            in_s[e, p * ROWS:(p + 1) * ROWS, pl.ds(b * BLOCK, BLOCK), :] = y
            return carry

        lax.fori_loop(0, blocks, step, 0, unroll=4)

    def channel_pair(a, at):
        x = recv[a, :, at:at + 16, :].astype(F32).reshape(n, 2, ROWS, width)
        return [x[:, h].reshape(width, width).astype(BF16) for h in range(2)]

    def put_pair(a, at, items):
        x = jnp.concatenate([item.reshape(n, ROWS, width) for item in items], axis=1)
        send[a, :, at:at + 16, :] = x.astype(BF16)

    def triangle(t, la, ra, pa):
        for cc in range(2):
            channels_here(cc, (la, ra))
            for cp in range(cc * group // 4, (cc + 1) * group // 4):
                left, right = channel_pair(la, cp * 16), channel_pair(ra, cp * 16)
                items = []
                for h in range(2):
                    mats_s[t, 0, 2 * cp + h] = left[h]
                    mats_s[t, 1, 2 * cp + h] = right[h]
                    items.append(nt(left[h], right[h]) if t == 0 else tn(left[h], right[h]))
                put_pair(pa, cp * 16, items)
            to_pairs(cc, (pa,))

    def triangle_back(t, da, la, ra):
        for cc in range(2):
            channels_here(cc, (da,))
            for cp in range(cc * group // 4, (cc + 1) * group // 4):
                grads = channel_pair(da, cp * 16)
                dl, dr = [], []
                for h in range(2):
                    left, right = mats_s[t, 0, 2 * cp + h], mats_s[t, 1, 2 * cp + h]
                    if t == 0:
                        dl.append(nn(grads[h], right))
                        dr.append(tn(grads[h], left))
                    else:
                        dl.append(nt(right, grads[h]))
                        dr.append(nn(left, grads[h]))
                put_pair(la, cp * 16, dl)
                put_pair(ra, cp * 16, dr)
            to_pairs(cc, (la, ra))

    def front(t, q, z):
        normed, inv = norm(z.astype(F32))
        nb = normed.astype(BF16)
        nrm_s[t, q], istd_s[t, q], nb_s[t, q] = normed, inv, nb
        make_edge(t, 0, q, nb)

    def make_edge(t, e, q, nb):
        both = nn(pwt_s[t, 2 * e * CH:(2 * e + 2) * CH, :], nb)
        scale = pm_s[pl.ds(q, 1), :] * sigmoid(both[CH:])
        edge = scale * both[:CH]
        side_s[t, 2 * e, q] = scale
        side_s[t, 2 * e + 1, q] = edge
        edge_s[e, q] = edge.astype(BF16)

    def gates(t):
        def step(q, carry):
            gate_s[t, q] = sigmoid(nn(pwt_s[t, 4 * CH:5 * CH, :], nb_s[t, q]))
            return carry

        lax.fori_loop(0, 2 * ROWS, step, 0, unroll=8)

    def rear(t, q):
        normed, inv = norm(in_s[0, q])
        nb = normed.astype(BF16)
        update = nn(owt_s[t], nb)
        pn_s[t, q], pstd_s[t, q], pnb_s[t, q], upd_s[t, q] = normed, inv, nb, update
        return (z_s[t, q].astype(F32) + gate_s[t, q] * update).astype(BF16)

    def rear_back(t, q, up):
        gate = gate_s[t, q]
        dupd = (up * gate).astype(BF16)
        dupd_s[t, q] = dupd
        g = nn(ow_ref[t], dupd)
        edge_s[0, q] = norm_back(pn_s[t, q], pstd_s[t, q], g).astype(BF16)

    def gate_back(t, q, up):
        gate = gate_s[t, q]
        dproj_s[t, q, 4 * CH:5 * CH, :] = (up * upd_s[t, q] * gate * (1.0 - gate)).astype(BF16)

    def edge_back(t, e, q):
        grad, scale = in_s[e, q], side_s[t, 2 * e, q]
        dproj_s[t, q, 2 * e * CH:(2 * e + 1) * CH, :] = (grad * scale).astype(BF16)
        dproj_s[t, q, (2 * e + 1) * CH:(2 * e + 2) * CH, :] = (
            grad * side_s[t, 2 * e + 1, q] * (1.0 - scale)
        ).astype(BF16)

    def front_back(t, q, up):
        h = nn(pw_ref[t], dproj_s[t, q])
        return (up + norm_back(nrm_s[t, q], istd_s[t, q], h)).astype(BF16)

    early_rows, late_rows = 8 * CH // n, 4 * CH // n

    def out_grad(t):
        total = nt(pnb_s[t, 0], dupd_s[t, 0])
        for q in range(1, 2 * ROWS):
            total += nt(pnb_s[t, q], dupd_s[t, q])
        return total

    def proj_grad(t, b, p=None):
        first, last = (0, 2 * ROWS) if p is None else (p * ROWS, (p + 1) * ROWS)
        total = nt(nb_s[t, first], dproj_s[t, first, b * CH:(b + 1) * CH, :])
        for q in range(first + 1, last):
            total += nt(nb_s[t, q], dproj_s[t, q, b * CH:(b + 1) * CH, :])
        return total

    def piece(at, size):
        return pl.ds(pl.multiple_of(at * size, size), size)

    def scatter(g, r, size, k):
        r[me] = g[piece(me, size), :]

        def go(to):
            pltpu.make_async_remote_copy(
                src_ref=g.at[piece(to, size)], dst_ref=r.at[me],
                send_sem=gsend_sem.at[k], recv_sem=grecv_sem.at[k],
                device_id={"dap": to}, device_id_type=MESH,
            ).start()

        to_all(go)

    def spread(x, r, k):
        def go(to):
            pltpu.make_async_remote_copy(
                src_ref=x, dst_ref=r.at[me], send_sem=gsend_sem.at[k], recv_sem=grecv_sem.at[k],
                device_id={"dap": to}, device_id_type=MESH,
            ).start()

        to_all(go)

    def across(x, y, k):
        y[mine] = x[...]
        for t in range(1, dp):
            pltpu.make_async_remote_copy(
                src_ref=x, dst_ref=y.at[mine], send_sem=gsend_sem.at[k], recv_sem=grecv_sem.at[k],
                device_id={"dp": lax.rem(mine + t, dp)}, device_id_type=MESH,
            ).start()

    def bulk(r, count, k):
        return pltpu.make_async_remote_copy(
            src_ref=r.at[pl.ds(0, count)], dst_ref=r.at[pl.ds(0, count)],
            send_sem=gsend_sem.at[k], recv_sem=grecv_sem.at[k],
            device_id={"dap": lax.rem(me + 1, n)}, device_id_type=MESH,
        )

    def summed(r, count):
        total = r[0].astype(F32)
        for t in range(1, count):
            total += r[t].astype(F32)
        return total

    inverse = 1.0 / (dp * width)

    def loop(body, p):
        def step(i, carry):
            body(i, i + p * ROWS)
            return carry

        lax.fori_loop(0, ROWS, step, 0, unroll=8)

    loads[4].wait()
    for p in range(2):
        def begin(i, q):
            x = nt(eye_s[...], pair_ref[i, p * half:(p + 1) * half, :])
            z = (x + sc_s[pl.ds(q, 1), :] * bias_s[...]).astype(BF16)
            z_s[0, q] = z
            front(0, q, z)

        def begin_right(i, q):
            make_edge(0, 1, q, nb_s[0, q])

        loop(begin, p)
        pack(p, L1, 0)
        if p == 0:
            pl.semaphore_wait(barrier, n - 1 + dp - 1)
            to_channels(0, (L1,))
        loop(begin_right, p)
        pack(p, R1, 1)
        to_channels(p, (R1,) if p == 0 else (L1, R1))
    loads[5].wait()
    loads[6].wait()
    turn_weight(0, 4)
    for b in range(5):
        turn_weight(1, b)
    for t in range(2):
        owt_s[t] = nt(eye_s[...], ow_ref[t]).astype(BF16)
    pt_s[...] = one_hot(256, 256, lambda r, q: q == (r % BLOCK) * ROWS + r // BLOCK).astype(BF16)
    gates(0)
    for p in range(2):
        def turn(i, q):
            cot_s[q] = nt(eye_s[...], cot_ref[i, p * half:(p + 1) * half, :]).astype(BF16)

        loop(turn, p)
    triangle(0, L1, R1, P1)
    for p in range(2):
        def middle(i, q):
            z = rear(0, q)
            z_s[1, q] = z
            front(1, q, z)

        pairs_here(p, P1)
        unpack(p, P1, 0)
        def middle_right(i, q):
            make_edge(1, 1, q, nb_s[1, q])

        loop(middle, p)
        pack(p, L2, 0)
        if p == 0:
            to_channels(0, (L2,))
        loop(middle_right, p)
        pack(p, R2, 1)
        to_channels(p, (R2,) if p == 0 else (L2, R2))
    gates(1)
    triangle(1, L2, R2, P2)

    for p in range(2):
        def last(i, q):
            z_s[2, q] = rear(1, q)
            rear_back(1, q, cot_s[q].astype(F32))

        pairs_here(p, P2)
        unpack(p, P2, 0)
        loop(last, p)
        pack(p, DP2, 0)
        to_channels(p, (DP2,))
    for p in range(2):
        def write_out(i, q):
            outv_s[i, p * half:(p + 1) * half, :] = nt(eye_s[0:half, 0:half], z_s[2, q]).astype(BF16)

        def gate_two(i, q):
            gate_back(1, q, cot_s[q].astype(F32))

        loop(write_out, p)
        loop(gate_two, p)
    put_out = pltpu.make_async_copy(outv_s, out_ref, put_sem.at[0])
    put_out.start()
    ge_s[5 * CH:6 * CH, :] = out_grad(1).astype(BF16)
    triangle_back(1, DP2, DL2, DR2)
    ge_s[4 * CH:5 * CH, :] = proj_grad(1, 4).astype(BF16)

    for p in range(2):
        def back(i, q):
            edge_back(1, 1, q)
            grad = front_back(1, q, cot_s[q].astype(F32))
            dz_s[0, q] = grad
            rear_back(0, q, grad.astype(F32))

        def back_left(i, q):
            edge_back(1, 0, q)

        pairs_here(p, DL2)
        unpack(p, DL2, 0)
        loop(back_left, p)
        pairs_here(p, DR2)
        unpack(p, DR2, 1)
        loop(back, p)
        pack(p, DP1, 0)
        to_channels(p, (DP1,))
    for b in range(4):
        ge_s[b * CH:(b + 1) * CH, :] = proj_grad(1, b).astype(BF16)
    for p in range(2):
        def gate_one(i, q):
            gate_back(0, q, dz_s[0, q].astype(F32))

        loop(gate_one, p)
    ge_s[6 * CH:7 * CH, :] = proj_grad(0, 4).astype(BF16)
    ge_s[7 * CH:8 * CH, :] = out_grad(0).astype(BF16)
    scatter(ge_s, re_s, early_rows, 0)
    triangle_back(0, DP1, DL1, DR1)
    bulk(re_s, n - 1, 0).wait_recv()
    xe_s[...] = summed(re_s, n)
    across(xe_s, ye_s, 1)
    chain_s[...] = jnp.zeros_like(chain_s)
    for p in range(2):
        for e in range(2):
            def end(i, q):
                edge_back(0, e, q)

            pairs_here(p, (DL1, DR1)[e])
            unpack(p, (DL1, DR1)[e], e)
            loop(end, p)
            for b in (2 * e, 2 * e + 1):
                if p == 0:
                    acc_s[b] = proj_grad(0, b, 0)
                else:
                    gf_s[b * CH:(b + 1) * CH, :] = (acc_s[b] + proj_grad(0, b, 1)).astype(BF16)
        if p == 0:
            bulk(ye_s, dp - 1, 1).wait_recv()
            ae_s[me] = (summed(ye_s, dp) * inverse).astype(BF16)
            spread(ae_s.at[me], ae_s, 2)
    scatter(gf_s, rf_s, late_rows, 3)
    for p in range(2):
        def finish(i, q):
            grad = front_back(0, q, dz_s[0, q].astype(F32))
            dz_s[1, q] = grad
            chain_s[...] += grad.astype(F32) * sc_s[pl.ds(q, 1), :]

        loop(finish, p)
    column_sum = jnp.sum(chain_s[...], axis=1, keepdims=True)
    cg_s[...] = jnp.sum(diag * column_sum, axis=0, keepdims=True)
    cr_s[me] = cg_s[...]
    spread(cg_s, cr_s, 6)
    bulk(rf_s, n - 1, 3).wait_recv()
    xf_s[...] = summed(rf_s, n)
    across(xf_s, yf_s, 4)
    for p in range(2):
        def write_grad(i, q):
            pgv_s[i, p * half:(p + 1) * half, :] = nt(eye_s[0:half, 0:half], dz_s[1, q]).astype(BF16)

        loop(write_grad, p)
    put_grad = pltpu.make_async_copy(pgv_s, pg_ref, put_sem.at[1])
    put_grad.start()
    bulk(cr_s, n - 1, 6).wait_recv()
    cx_s[...] = summed(cr_s, n)
    across(cx_s, cy_s, 7)
    bulk(yf_s, dp - 1, 4).wait_recv()
    af_s[me] = (summed(yf_s, dp) * inverse).astype(BF16)
    spread(af_s.at[me], af_s, 5)
    bulk(ae_s, n - 1, 2).wait_recv()
    full = ae_s[...].reshape(8 * CH, CH).astype(F32)
    for b in range(5):
        gproj_ref[1, :, b * CH:(b + 1) * CH] = full[b * CH:(b + 1) * CH]
    gout_ref[1] = full[5 * CH:6 * CH]
    gproj_ref[0, :, 4 * CH:5 * CH] = full[6 * CH:7 * CH]
    gout_ref[0] = full[7 * CH:8 * CH]
    bulk(cy_s, dp - 1, 7).wait_recv()
    gchain_ref[...] = summed(cy_s, dp) * inverse

    def drain(a, carry):
        sent(a)
        return carry

    lax.fori_loop(0, 12, drain, 0)
    for r, count, k in ((re_s, n, 0), (ye_s, dp, 1), (ae_s, n, 2), (rf_s, n, 3), (yf_s, dp, 4), (cr_s, n, 6), (cy_s, dp, 7)):
        bulk(r, count - 1, k).wait_send()
    put_out.wait()
    put_grad.wait()
    bulk(af_s, n - 1, 5).wait_recv()
    full = af_s[...].reshape(4 * CH, CH).astype(F32)
    for b in range(4):
        gproj_ref[0, :, b * CH:(b + 1) * CH] = full[b * CH:(b + 1) * CH]
    bulk(af_s, n - 1, 5).wait_send()


def hand_over(*refs):
    count = (len(refs) - 2) // 3
    given, outs, held = refs[:count], refs[count:2 * count], refs[2 * count:3 * count]
    in_sem, out_sem = refs[-2:]
    parts = []
    for k in range(count):
        lead = given[k].shape[0]
        step = max(1, lead // 4)
        parts += [(k, pl.ds(at, step)) for at in range(0, lead, step)]
    fetched = [
        pltpu.make_async_copy(given[k].at[at], held[k].at[at], in_sem.at[m]) for m, (k, at) in enumerate(parts)
    ]
    put = [
        pltpu.make_async_copy(held[k].at[at], outs[k].at[at], out_sem.at[m]) for m, (k, at) in enumerate(parts)
    ]
    for copy in fetched:
        copy.start()
    for m in range(len(parts)):
        fetched[m].wait()
        put[m].start()
    for copy in put:
        copy.wait()


def body(n, dp, pair_in, residue_mask, chain_index, chain_bias, proj_weight, out_weight, cotangent):
    width = n * ROWS
    group = CH // n
    early_rows, late_rows = 8 * CH // n, 4 * CH // n
    tensor = (2 * ROWS, CH, width // 2)
    line = (2 * ROWS, 1, width // 2)
    vmem = pl.BlockSpec(memory_space=pltpu.VMEM)
    shapes = [
        jax.ShapeDtypeStruct((ROWS, width, CH), BF16),
        jax.ShapeDtypeStruct((ROWS, width, CH), BF16),
        jax.ShapeDtypeStruct((2, CH, 5 * CH), F32),
        jax.ShapeDtypeStruct((2, CH, CH), F32),
        jax.ShapeDtypeStruct((1, CH), F32),
    ]
    scratch = [
        pltpu.VMEM((ROWS, width, CH), BF16),
        pltpu.VMEM((1, width), jnp.int32),
        pltpu.VMEM((1, width), jnp.int32),
        pltpu.VMEM((1, CH), F32),
        pltpu.VMEM((2, CH, 5 * CH), BF16),
        pltpu.VMEM((2, CH, CH), BF16),
        pltpu.VMEM((ROWS, width, CH), BF16),
        pltpu.SemaphoreType.DMA((7,)),
        pltpu.VMEM((CH, CH), BF16),
        pltpu.VMEM((256, 256), BF16),
        pltpu.VMEM((256, 256), BF16),
        pltpu.VMEM((2, 5 * CH, CH), BF16),
        pltpu.VMEM((2, CH, CH), BF16),
        pltpu.VMEM((CH, 1), F32),
        pltpu.VMEM((2 * ROWS, width // 2), F32),
        pltpu.VMEM((2 * ROWS, width // 2), F32),
        pltpu.VMEM((3,) + tensor, BF16),
        pltpu.VMEM(tensor, BF16),
        pltpu.VMEM((2,) + tensor, BF16),
        pltpu.VMEM((2,) + tensor, BF16),
        pltpu.VMEM((2,) + tensor, F32),
        pltpu.VMEM((2,) + line, F32),
        pltpu.VMEM((2, 4) + tensor, F32),
        pltpu.VMEM((2,) + tensor, F32),
        pltpu.VMEM((2,) + tensor, F32),
        pltpu.VMEM((2,) + tensor, BF16),
        pltpu.VMEM((2,) + line, F32),
        pltpu.VMEM((2,) + tensor, F32),
        pltpu.VMEM((2,) + tensor, BF16),
        pltpu.VMEM((2, 2 * ROWS, 5 * CH, width // 2), BF16),
        pltpu.VMEM((2,) + tensor, BF16),
        pltpu.VMEM((2,) + tensor, F32),
        pltpu.VMEM((2, 2, group, width, width), BF16),
        pltpu.VMEM((CH, width // 2), F32),
        pltpu.VMEM((4, CH, CH), F32),
        pltpu.VMEM((12, n, group * ROWS, width), BF16),
        pltpu.VMEM((12, n, group * ROWS, width), BF16),
        pltpu.VMEM((8 * CH, CH), BF16),
        pltpu.VMEM((n, early_rows, CH), BF16),
        pltpu.VMEM((n, early_rows, CH), BF16),
        pltpu.VMEM((4 * CH, CH), BF16),
        pltpu.VMEM((n, late_rows, CH), BF16),
        pltpu.VMEM((n, late_rows, CH), BF16),
        pltpu.VMEM((early_rows, CH), F32),
        pltpu.VMEM((dp, early_rows, CH), F32),
        pltpu.VMEM((late_rows, CH), F32),
        pltpu.VMEM((dp, late_rows, CH), F32),
        pltpu.VMEM((1, CH), F32),
        pltpu.VMEM((n, 1, CH), F32),
        pltpu.VMEM((1, CH), F32),
        pltpu.VMEM((dp, 1, CH), F32),
        pltpu.VMEM((ROWS, width, CH), BF16),
        pltpu.VMEM((ROWS, width, CH), BF16),
        pltpu.SemaphoreType.DMA((12,)),
        pltpu.SemaphoreType.DMA((12, 3)),
        pltpu.SemaphoreType.DMA((8,)),
        pltpu.SemaphoreType.DMA((8,)),
        pltpu.SemaphoreType.DMA((2,)),
    ]
    results = pl.pallas_call(
        functools.partial(kernel, n, dp),
        out_shape=shapes,
        in_specs=[pl.BlockSpec(memory_space=pl.ANY)] * 7,
        out_specs=[pl.BlockSpec(memory_space=pl.ANY)] * 2 + [vmem] * 3,
        scratch_shapes=scratch,
        compiler_params=pltpu.CompilerParams(
            collective_id=0, has_side_effects=True, vmem_limit_bytes=62 * 1024 * 1024
        ),
    )(
        pair_in[0], residue_mask, chain_index, chain_bias.reshape(1, CH),
        proj_weight, out_weight, cotangent[0],
    )
    anywhere = pl.BlockSpec(memory_space=pl.ANY)
    out_pair, pair_grad, grad_proj, grad_out, grad_chain = pl.pallas_call(
        hand_over,
        out_shape=shapes,
        in_specs=[anywhere] * 5,
        out_specs=[anywhere] * 5,
        scratch_shapes=[pltpu.VMEM(shape.shape, shape.dtype) for shape in shapes]
        + [pltpu.SemaphoreType.DMA((13,)), pltpu.SemaphoreType.DMA((13,))],
        compiler_params=pltpu.CompilerParams(vmem_limit_bytes=62 * 1024 * 1024),
    )(*results)
    return out_pair[None], pair_grad[None], grad_proj, grad_out, grad_chain.reshape(CH)


def solution(mesh):
    n, dp = mesh.shape["dap"], mesh.shape["dp"]
    rows = P("dp", "dap", None, None)
    return jax.shard_map(
        functools.partial(body, n, dp),
        mesh=mesh,
        in_specs=(rows, P("dp", None), P("dp", None), P(), P(), P(), rows),
        out_specs=(rows, rows, P(), P(), P()),
        check_vma=False,
    )
```

```python
import functools

import jax
import jax.numpy as jnp
from jax import lax
from jax.experimental import pallas as pl
from jax.experimental.pallas import tpu as pltpu
from jax.sharding import PartitionSpec as P

EPSILON = 1e-05
MESH = pl.DeviceIdType.MESH
F32 = jnp.float32
BF16 = jnp.bfloat16
ROWS = 8
CH = 128
BLOCK = 32

L1, R1, P1, L2, R2, P2, DP2, DL2, DR2, DP1, DL1, DR1 = range(12)


def nt(a, b):
    return lax.dot_general(a, b, (((1,), (1,)), ((), ())), preferred_element_type=F32)


def tn(a, b):
    return lax.dot_general(a, b, (((0,), (0,)), ((), ())), preferred_element_type=F32)


def nn(a, b):
    return jnp.dot(a, b, preferred_element_type=F32)


def one_hot(rows, columns, wanted):
    r = lax.broadcasted_iota(jnp.int32, (rows, columns), 0)
    q = lax.broadcasted_iota(jnp.int32, (rows, columns), 1)
    return jnp.where(wanted(r, q), 1.0, 0.0).astype(F32)


def sigmoid(x):
    return 0.5 * jnp.tanh(0.5 * x) + 0.5


def norm(x):
    centred = x - jnp.mean(x, axis=0, keepdims=True)
    inv = lax.rsqrt(jnp.mean(centred * centred, axis=0, keepdims=True) + EPSILON)
    return centred * inv, inv


def norm_back(normed, inv, g):
    first = jnp.mean(g, axis=0, keepdims=True)
    second = jnp.mean(g * normed, axis=0, keepdims=True)
    return (g - first - normed * second) * inv


def kernel(
    n, dp, pair_in, mask_in, chain_in, bias_in, pw_in, ow_in, cot_in,
    out_ref, pg_ref, gproj_ref, gout_ref, gchain_ref,
    pair_ref, mask_ref, chain_ref, bias_ref, pw_ref, ow_ref, cot_ref, load_sem,
    eye_s, pf_s, pt_s, pwt_s, owt_s, bias_s, pm_s, sc_s,
    z_s, cot_s, dz_s, nb_s, nrm_s, istd_s, side_s, gate_s, pn_s, pnb_s, pstd_s, upd_s,
    dupd_s, dproj_s, edge_s, in_s, mats_s, chain_s, acc_s,
    send, recv, ge_s, re_s, ae_s, gf_s, rf_s, af_s, xe_s, ye_s, xf_s, yf_s, cg_s, cr_s, cx_s, cy_s, outv_s, pgv_s,
    send_sem, recv_sem, gsend_sem, grecv_sem, put_sem,
):
    width = n * ROWS
    half = width // 2
    group = CH // n
    rows = group * ROWS
    half_rows = rows // 2
    per = BLOCK * ROWS // rows
    blocks = CH // BLOCK
    me = lax.axis_index("dap")
    mine = lax.axis_index("dp")

    pairs = (
        (bias_in, bias_ref), (mask_in, mask_ref), (chain_in, chain_ref), (pw_in, pw_ref),
        (pair_in, pair_ref), (ow_in, ow_ref), (cot_in, cot_ref),
    )
    loads = [pltpu.make_async_copy(given, held, load_sem.at[k]) for k, (given, held) in enumerate(pairs)]
    for load in loads:
        load.start()
    barrier = pltpu.get_barrier_semaphore()

    def greet(t, carry):
        pl.semaphore_signal(barrier, inc=1, device_id={"dap": lax.rem(me + t, n)}, device_id_type=MESH)
        return carry

    lax.fori_loop(1, n, greet, 0)

    def greet_dp(t, carry):
        pl.semaphore_signal(barrier, inc=1, device_id={"dp": lax.rem(mine + t, dp)}, device_id_type=MESH)
        return carry

    lax.fori_loop(1, dp, greet_dp, 0)

    eye_s[...] = one_hot(CH, CH, lambda r, q: r == q).astype(BF16)
    pf_s[...] = one_hot(256, 256, lambda r, q: q == (r % ROWS) * BLOCK + r // ROWS).astype(BF16)
    diag = one_hot(CH, CH, lambda r, q: r == q)
    for load in loads[:4]:
        load.wait()
    bias_s[...] = jnp.sum(diag * bias_ref[...], axis=1, keepdims=True)

    def turn_weight(t, b):
        pwt_s[t, b * CH:(b + 1) * CH, :] = nt(eye_s[...], pw_ref[t, :, b * CH:(b + 1) * CH]).astype(BF16)

    for b in range(4):
        turn_weight(0, b)
    live = mask_ref[...].astype(F32)
    chain = chain_ref[...].astype(F32)
    own = one_hot(ROWS, width, lambda r, q: q == r + ROWS * me)
    pair_mask = jnp.sum(own * live, axis=1, keepdims=True) * live
    same = jnp.where(jnp.sum(own * chain, axis=1, keepdims=True) == chain, 1.0, 0.0)
    for p in range(2):
        pm_s[p * ROWS:(p + 1) * ROWS, :] = pair_mask[:, p * half:(p + 1) * half]
        sc_s[p * ROWS:(p + 1) * ROWS, :] = same[:, p * half:(p + 1) * half]

    if n == 32:
        row, plane, column = me // 8, (me // 4) % 2, me % 4
        planes = [4 * lax.rem(plane + k, 2) for k in range(2)]
        columns = [lax.rem(column + k, 4) for k in range(4)]

    def to_all(start):
        if n != 32:
            lax.fori_loop(1, n, lambda t, carry: (start(lax.rem(me + t, n)), carry)[1], 0)
            return

        lines = [8 * lax.rem(row + k, 4) for k in range(4)]
        away = (0, 1, 2, 1)
        order = [(k, h, c) for k in range(4) for h in range(2) for c in range(4)]
        order.sort(key=lambda d: (-(away[d[0]] + d[1] + away[d[2]]), (d[0] + 2 * d[2] + d[1]) % 4))
        for k, h, c in order[:-1]:
            start(lines[k] + planes[h] + columns[c])

    def push(messages):
        for a, r0, rn, p, k in messages:
            at = (a, pl.ds(me, 1), slice(r0, r0 + rn), slice(p * half, (p + 1) * half))
            recv[at] = send[at]

        def go(to):
            for a, r0, rn, p, k in messages:
                part = (pl.ds(r0, rn), pl.ds(p * half, half))
                pltpu.make_async_remote_copy(
                    src_ref=send.at[(a, to) + part], dst_ref=recv.at[(a, me) + part],
                    send_sem=send_sem.at[a], recv_sem=recv_sem.at[a, k],
                    device_id={"dap": to}, device_id_type=MESH,
                ).start()

        to_all(go)

    def arrived(a, r0, rn, p, k):
        part = (a, pl.ds(0, n - 1), pl.ds(r0, rn), pl.ds(p * half, half))
        pltpu.make_async_remote_copy(
            src_ref=send.at[part], dst_ref=recv.at[part],
            send_sem=send_sem.at[a], recv_sem=recv_sem.at[a, k],
            device_id={"dap": lax.rem(me + 1, n)}, device_id_type=MESH,
        ).wait_recv()

    def sent(a):
        part = (a, pl.ds(0, n - 1))
        pltpu.make_async_remote_copy(
            src_ref=send.at[part], dst_ref=recv.at[part],
            send_sem=send_sem.at[a], recv_sem=recv_sem.at[a, 0],
            device_id={"dap": lax.rem(me + 1, n)}, device_id_type=MESH,
        ).wait_send()

    def to_channels(p, items):
        if p == 0:
            push([(a, 0, rows, 0, 0) for a in items])
        else:
            push([(a, 0, half_rows, 1, 1) for a in items])
            push([(a, half_rows, half_rows, 1, 2) for a in items])

    def channels_here(cc, items):
        for a in items:
            if cc == 0:
                arrived(a, 0, rows, 0, 0)
            arrived(a, cc * half_rows, half_rows, 1, 1 + cc)

    def to_pairs(cc, items):
        push([(a, cc * half_rows, half_rows, 0, 0) for a in items])
        if cc == 1:
            for a in items:
                push([(a, 0, rows, 1, 1)])

    def pairs_here(p, a):
        arrived(a, 0, rows, p, p)

    def pack(p, a, e):
        def step(b, carry):
            x = edge_s[e, p * ROWS:(p + 1) * ROWS, pl.ds(b * BLOCK, BLOCK), :].reshape(256, half)
            y = nn(pf_s[...], x).astype(BF16)
            send[a, pl.ds(b * per, per), :, p * half:(p + 1) * half] = y.reshape(per, rows, half)
            return carry

        lax.fori_loop(0, blocks, step, 0, unroll=4)

    def unpack(p, a, e):
        def step(b, carry):
            x = recv[a, pl.ds(b * per, per), :, p * half:(p + 1) * half].reshape(256, half)
            y = nn(pt_s[...], x).reshape(ROWS, BLOCK, half)
            in_s[e, p * ROWS:(p + 1) * ROWS, pl.ds(b * BLOCK, BLOCK), :] = y
            return carry

        lax.fori_loop(0, blocks, step, 0, unroll=4)

    def channel_pair(a, at):
        x = recv[a, :, at:at + 16, :].astype(F32).reshape(n, 2, ROWS, width)
        return [x[:, h].reshape(width, width).astype(BF16) for h in range(2)]

    def put_pair(a, at, items):
        x = jnp.concatenate([item.reshape(n, ROWS, width) for item in items], axis=1)
        send[a, :, at:at + 16, :] = x.astype(BF16)

    def triangle(t, la, ra, pa):
        for cc in range(2):
            channels_here(cc, (la, ra))
            for cp in range(cc * group // 4, (cc + 1) * group // 4):
                left, right = channel_pair(la, cp * 16), channel_pair(ra, cp * 16)
                items = []
                for h in range(2):
                    mats_s[t, 0, 2 * cp + h] = left[h]
                    mats_s[t, 1, 2 * cp + h] = right[h]
                    items.append(nt(left[h], right[h]) if t == 0 else tn(left[h], right[h]))
                put_pair(pa, cp * 16, items)
            to_pairs(cc, (pa,))

    def triangle_back(t, da, la, ra):
        for cc in range(2):
            channels_here(cc, (da,))
            for cp in range(cc * group // 4, (cc + 1) * group // 4):
                grads = channel_pair(da, cp * 16)
                dl, dr = [], []
                for h in range(2):
                    left, right = mats_s[t, 0, 2 * cp + h], mats_s[t, 1, 2 * cp + h]
                    if t == 0:
                        dl.append(nn(grads[h], right))
                        dr.append(tn(grads[h], left))
                    else:
                        dl.append(nt(right, grads[h]))
                        dr.append(nn(left, grads[h]))
                put_pair(la, cp * 16, dl)
                put_pair(ra, cp * 16, dr)
            to_pairs(cc, (la, ra))

    def front(t, q, z):
        normed, inv = norm(z.astype(F32))
        nb = normed.astype(BF16)
        nrm_s[t, q], istd_s[t, q], nb_s[t, q] = normed, inv, nb
        make_edge(t, 0, q, nb)

    def make_edge(t, e, q, nb):
        both = nn(pwt_s[t, 2 * e * CH:(2 * e + 2) * CH, :], nb)
        scale = pm_s[pl.ds(q, 1), :] * sigmoid(both[CH:])
        edge = scale * both[:CH]
        side_s[t, 2 * e, q] = scale
        side_s[t, 2 * e + 1, q] = edge
        edge_s[e, q] = edge.astype(BF16)

    def gates(t):
        def step(q, carry):
            gate_s[t, q] = sigmoid(nn(pwt_s[t, 4 * CH:5 * CH, :], nb_s[t, q]))
            return carry

        lax.fori_loop(0, 2 * ROWS, step, 0, unroll=8)

    def rear(t, q):
        normed, inv = norm(in_s[0, q])
        nb = normed.astype(BF16)
        update = nn(owt_s[t], nb)
        pn_s[t, q], pstd_s[t, q], pnb_s[t, q], upd_s[t, q] = normed, inv, nb, update
        return (z_s[t, q].astype(F32) + gate_s[t, q] * update).astype(BF16)

    def rear_back(t, q, up):
        gate = gate_s[t, q]
        dupd = (up * gate).astype(BF16)
        dupd_s[t, q] = dupd
        g = nn(ow_ref[t], dupd)
        edge_s[0, q] = norm_back(pn_s[t, q], pstd_s[t, q], g).astype(BF16)

    def gate_back(t, q, up):
        gate = gate_s[t, q]
        dproj_s[t, q, 4 * CH:5 * CH, :] = (up * upd_s[t, q] * gate * (1.0 - gate)).astype(BF16)

    def edge_back(t, e, q):
        grad, scale = in_s[e, q], side_s[t, 2 * e, q]
        dproj_s[t, q, 2 * e * CH:(2 * e + 1) * CH, :] = (grad * scale).astype(BF16)
        dproj_s[t, q, (2 * e + 1) * CH:(2 * e + 2) * CH, :] = (
            grad * side_s[t, 2 * e + 1, q] * (1.0 - scale)
        ).astype(BF16)

    def front_back(t, q, up):
        h = nn(pw_ref[t], dproj_s[t, q])
        return (up + norm_back(nrm_s[t, q], istd_s[t, q], h)).astype(BF16)

    early_rows, late_rows = 8 * CH // n, 4 * CH // n

    def out_grad(t):
        total = nt(pnb_s[t, 0], dupd_s[t, 0])
        for q in range(1, 2 * ROWS):
            total += nt(pnb_s[t, q], dupd_s[t, q])
        return total

    def proj_grad(t, b, p=None):
        first, last = (0, 2 * ROWS) if p is None else (p * ROWS, (p + 1) * ROWS)
        total = nt(nb_s[t, first], dproj_s[t, first, b * CH:(b + 1) * CH, :])
        for q in range(first + 1, last):
            total += nt(nb_s[t, q], dproj_s[t, q, b * CH:(b + 1) * CH, :])
        return total

    def piece(at, size):
        return pl.ds(pl.multiple_of(at * size, size), size)

    def scatter(g, r, size, k):
        r[me] = g[piece(me, size), :]

        def go(to):
            pltpu.make_async_remote_copy(
                src_ref=g.at[piece(to, size)], dst_ref=r.at[me],
                send_sem=gsend_sem.at[k], recv_sem=grecv_sem.at[k],
                device_id={"dap": to}, device_id_type=MESH,
            ).start()

        to_all(go)

    def spread(x, r, k):
        def go(to):
            pltpu.make_async_remote_copy(
                src_ref=x, dst_ref=r.at[me], send_sem=gsend_sem.at[k], recv_sem=grecv_sem.at[k],
                device_id={"dap": to}, device_id_type=MESH,
            ).start()

        to_all(go)

    def across(x, y, k):
        y[mine] = x[...]
        for t in range(1, dp):
            pltpu.make_async_remote_copy(
                src_ref=x, dst_ref=y.at[mine], send_sem=gsend_sem.at[k], recv_sem=grecv_sem.at[k],
                device_id={"dp": lax.rem(mine + t, dp)}, device_id_type=MESH,
            ).start()

    def bulk(r, count, k):
        return pltpu.make_async_remote_copy(
            src_ref=r.at[pl.ds(0, count)], dst_ref=r.at[pl.ds(0, count)],
            send_sem=gsend_sem.at[k], recv_sem=grecv_sem.at[k],
            device_id={"dap": lax.rem(me + 1, n)}, device_id_type=MESH,
        )

    def summed(r, count):
        total = r[0].astype(F32)
        for t in range(1, count):
            total += r[t].astype(F32)
        return total

    inverse = 1.0 / (dp * width)

    def loop(body, p):
        def step(i, carry):
            body(i, i + p * ROWS)
            return carry

        lax.fori_loop(0, ROWS, step, 0, unroll=8)

    loads[4].wait()
    for p in range(2):
        def begin(i, q):
            x = nt(eye_s[...], pair_ref[i, p * half:(p + 1) * half, :])
            z = (x + sc_s[pl.ds(q, 1), :] * bias_s[...]).astype(BF16)
            z_s[0, q] = z
            front(0, q, z)

        def begin_right(i, q):
            make_edge(0, 1, q, nb_s[0, q])

        loop(begin, p)
        pack(p, L1, 0)
        if p == 0:
            pl.semaphore_wait(barrier, n - 1 + dp - 1)
            to_channels(0, (L1,))
        loop(begin_right, p)
        pack(p, R1, 1)
        to_channels(p, (R1,) if p == 0 else (L1, R1))
    loads[5].wait()
    loads[6].wait()
    turn_weight(0, 4)
    for b in range(5):
        turn_weight(1, b)
    for t in range(2):
        owt_s[t] = nt(eye_s[...], ow_ref[t]).astype(BF16)
    pt_s[...] = one_hot(256, 256, lambda r, q: q == (r % BLOCK) * ROWS + r // BLOCK).astype(BF16)
    gates(0)
    for p in range(2):
        def turn(i, q):
            cot_s[q] = nt(eye_s[...], cot_ref[i, p * half:(p + 1) * half, :]).astype(BF16)

        loop(turn, p)
    triangle(0, L1, R1, P1)
    for p in range(2):
        def middle(i, q):
            z = rear(0, q)
            z_s[1, q] = z
            front(1, q, z)

        pairs_here(p, P1)
        unpack(p, P1, 0)
        def middle_right(i, q):
            make_edge(1, 1, q, nb_s[1, q])

        loop(middle, p)
        pack(p, L2, 0)
        if p == 0:
            to_channels(0, (L2,))
        loop(middle_right, p)
        pack(p, R2, 1)
        to_channels(p, (R2,) if p == 0 else (L2, R2))
    gates(1)
    triangle(1, L2, R2, P2)

    for p in range(2):
        def last(i, q):
            z_s[2, q] = rear(1, q)
            rear_back(1, q, cot_s[q].astype(F32))

        pairs_here(p, P2)
        unpack(p, P2, 0)
        loop(last, p)
        pack(p, DP2, 0)
        to_channels(p, (DP2,))
    for p in range(2):
        def write_out(i, q):
            outv_s[i, p * half:(p + 1) * half, :] = nt(eye_s[0:half, 0:half], z_s[2, q]).astype(BF16)

        def gate_two(i, q):
            gate_back(1, q, cot_s[q].astype(F32))

        loop(write_out, p)
        loop(gate_two, p)
    put_out = pltpu.make_async_copy(outv_s, out_ref, put_sem.at[0])
    put_out.start()
    ge_s[5 * CH:6 * CH, :] = out_grad(1).astype(BF16)
    triangle_back(1, DP2, DL2, DR2)
    ge_s[4 * CH:5 * CH, :] = proj_grad(1, 4).astype(BF16)

    for p in range(2):
        def back(i, q):
            edge_back(1, 1, q)
            grad = front_back(1, q, cot_s[q].astype(F32))
            dz_s[0, q] = grad
            rear_back(0, q, grad.astype(F32))

        def back_left(i, q):
            edge_back(1, 0, q)

        pairs_here(p, DL2)
        unpack(p, DL2, 0)
        loop(back_left, p)
        pairs_here(p, DR2)
        unpack(p, DR2, 1)
        loop(back, p)
        pack(p, DP1, 0)
        to_channels(p, (DP1,))
    for b in range(4):
        ge_s[b * CH:(b + 1) * CH, :] = proj_grad(1, b).astype(BF16)
    for p in range(2):
        def gate_one(i, q):
            gate_back(0, q, dz_s[0, q].astype(F32))

        loop(gate_one, p)
    ge_s[6 * CH:7 * CH, :] = proj_grad(0, 4).astype(BF16)
    ge_s[7 * CH:8 * CH, :] = out_grad(0).astype(BF16)
    scatter(ge_s, re_s, early_rows, 0)
    triangle_back(0, DP1, DL1, DR1)
    bulk(re_s, n - 1, 0).wait_recv()
    xe_s[...] = summed(re_s, n)
    across(xe_s, ye_s, 1)
    chain_s[...] = jnp.zeros_like(chain_s)
    for p in range(2):
        for e in range(2):
            def end(i, q):
                edge_back(0, e, q)

            pairs_here(p, (DL1, DR1)[e])
            unpack(p, (DL1, DR1)[e], e)
            loop(end, p)
            for b in (2 * e, 2 * e + 1):
                if p == 0:
                    acc_s[b] = proj_grad(0, b, 0)
                else:
                    gf_s[b * CH:(b + 1) * CH, :] = (acc_s[b] + proj_grad(0, b, 1)).astype(BF16)
        if p == 0:
            bulk(ye_s, dp - 1, 1).wait_recv()
            ae_s[me] = (summed(ye_s, dp) * inverse).astype(BF16)
            spread(ae_s.at[me], ae_s, 2)
    scatter(gf_s, rf_s, late_rows, 3)
    for p in range(2):
        def finish(i, q):
            grad = front_back(0, q, dz_s[0, q].astype(F32))
            dz_s[1, q] = grad
            chain_s[...] += grad.astype(F32) * sc_s[pl.ds(q, 1), :]

        loop(finish, p)
        if p == 0:
            bulk(rf_s, n - 1, 3).wait_recv()
            xf_s[...] = summed(rf_s, n)
            across(xf_s, yf_s, 4)
    column_sum = jnp.sum(chain_s[...], axis=1, keepdims=True)
    cg_s[...] = jnp.sum(diag * column_sum, axis=0, keepdims=True)
    cr_s[me] = cg_s[...]
    spread(cg_s, cr_s, 6)
    bulk(yf_s, dp - 1, 4).wait_recv()
    af_s[me] = (summed(yf_s, dp) * inverse).astype(BF16)
    spread(af_s.at[me], af_s, 5)
    for p in range(2):
        def write_grad(i, q):
            pgv_s[i, p * half:(p + 1) * half, :] = nt(eye_s[0:half, 0:half], dz_s[1, q]).astype(BF16)

        loop(write_grad, p)
    put_grad = pltpu.make_async_copy(pgv_s, pg_ref, put_sem.at[1])
    put_grad.start()
    bulk(cr_s, n - 1, 6).wait_recv()
    cx_s[...] = summed(cr_s, n)
    across(cx_s, cy_s, 7)
    bulk(ae_s, n - 1, 2).wait_recv()
    full = ae_s[...].reshape(8 * CH, CH).astype(F32)
    for b in range(5):
        gproj_ref[1, :, b * CH:(b + 1) * CH] = full[b * CH:(b + 1) * CH]
    gout_ref[1] = full[5 * CH:6 * CH]
    gproj_ref[0, :, 4 * CH:5 * CH] = full[6 * CH:7 * CH]
    gout_ref[0] = full[7 * CH:8 * CH]
    bulk(cy_s, dp - 1, 7).wait_recv()
    gchain_ref[...] = summed(cy_s, dp) * inverse

    def drain(a, carry):
        sent(a)
        return carry

    lax.fori_loop(0, 12, drain, 0)
    for r, count, k in ((re_s, n, 0), (ye_s, dp, 1), (ae_s, n, 2), (rf_s, n, 3), (yf_s, dp, 4), (cr_s, n, 6), (cy_s, dp, 7)):
        bulk(r, count - 1, k).wait_send()
    put_out.wait()
    put_grad.wait()
    bulk(af_s, n - 1, 5).wait_recv()
    full = af_s[...].reshape(4 * CH, CH).astype(F32)
    for b in range(4):
        gproj_ref[0, :, b * CH:(b + 1) * CH] = full[b * CH:(b + 1) * CH]
    bulk(af_s, n - 1, 5).wait_send()


def hand_over(*refs):
    count = (len(refs) - 2) // 3
    given, outs, held = refs[:count], refs[count:2 * count], refs[2 * count:3 * count]
    in_sem, out_sem = refs[-2:]
    parts = []
    for k in range(count):
        lead = given[k].shape[0]
        step = max(1, lead // 4)
        parts += [(k, pl.ds(at, step)) for at in range(0, lead, step)]
    fetched = [
        pltpu.make_async_copy(given[k].at[at], held[k].at[at], in_sem.at[m]) for m, (k, at) in enumerate(parts)
    ]
    put = [
        pltpu.make_async_copy(held[k].at[at], outs[k].at[at], out_sem.at[m]) for m, (k, at) in enumerate(parts)
    ]
    for copy in fetched:
        copy.start()
    for m in range(len(parts)):
        fetched[m].wait()
        put[m].start()
    for copy in put:
        copy.wait()


def body(n, dp, pair_in, residue_mask, chain_index, chain_bias, proj_weight, out_weight, cotangent):
    width = n * ROWS
    group = CH // n
    early_rows, late_rows = 8 * CH // n, 4 * CH // n
    tensor = (2 * ROWS, CH, width // 2)
    line = (2 * ROWS, 1, width // 2)
    vmem = pl.BlockSpec(memory_space=pltpu.VMEM)
    shapes = [
        jax.ShapeDtypeStruct((ROWS, width, CH), BF16),
        jax.ShapeDtypeStruct((ROWS, width, CH), BF16),
        jax.ShapeDtypeStruct((2, CH, 5 * CH), F32),
        jax.ShapeDtypeStruct((2, CH, CH), F32),
        jax.ShapeDtypeStruct((1, CH), F32),
    ]
    scratch = [
        pltpu.VMEM((ROWS, width, CH), BF16),
        pltpu.VMEM((1, width), jnp.int32),
        pltpu.VMEM((1, width), jnp.int32),
        pltpu.VMEM((1, CH), F32),
        pltpu.VMEM((2, CH, 5 * CH), BF16),
        pltpu.VMEM((2, CH, CH), BF16),
        pltpu.VMEM((ROWS, width, CH), BF16),
        pltpu.SemaphoreType.DMA((7,)),
        pltpu.VMEM((CH, CH), BF16),
        pltpu.VMEM((256, 256), BF16),
        pltpu.VMEM((256, 256), BF16),
        pltpu.VMEM((2, 5 * CH, CH), BF16),
        pltpu.VMEM((2, CH, CH), BF16),
        pltpu.VMEM((CH, 1), F32),
        pltpu.VMEM((2 * ROWS, width // 2), F32),
        pltpu.VMEM((2 * ROWS, width // 2), F32),
        pltpu.VMEM((3,) + tensor, BF16),
        pltpu.VMEM(tensor, BF16),
        pltpu.VMEM((2,) + tensor, BF16),
        pltpu.VMEM((2,) + tensor, BF16),
        pltpu.VMEM((2,) + tensor, F32),
        pltpu.VMEM((2,) + line, F32),
        pltpu.VMEM((2, 4) + tensor, F32),
        pltpu.VMEM((2,) + tensor, F32),
        pltpu.VMEM((2,) + tensor, F32),
        pltpu.VMEM((2,) + tensor, BF16),
        pltpu.VMEM((2,) + line, F32),
        pltpu.VMEM((2,) + tensor, F32),
        pltpu.VMEM((2,) + tensor, BF16),
        pltpu.VMEM((2, 2 * ROWS, 5 * CH, width // 2), BF16),
        pltpu.VMEM((2,) + tensor, BF16),
        pltpu.VMEM((2,) + tensor, F32),
        pltpu.VMEM((2, 2, group, width, width), BF16),
        pltpu.VMEM((CH, width // 2), F32),
        pltpu.VMEM((4, CH, CH), F32),
        pltpu.VMEM((12, n, group * ROWS, width), BF16),
        pltpu.VMEM((12, n, group * ROWS, width), BF16),
        pltpu.VMEM((8 * CH, CH), BF16),
        pltpu.VMEM((n, early_rows, CH), BF16),
        pltpu.VMEM((n, early_rows, CH), BF16),
        pltpu.VMEM((4 * CH, CH), BF16),
        pltpu.VMEM((n, late_rows, CH), BF16),
        pltpu.VMEM((n, late_rows, CH), BF16),
        pltpu.VMEM((early_rows, CH), F32),
        pltpu.VMEM((dp, early_rows, CH), F32),
        pltpu.VMEM((late_rows, CH), F32),
        pltpu.VMEM((dp, late_rows, CH), F32),
        pltpu.VMEM((1, CH), F32),
        pltpu.VMEM((n, 1, CH), F32),
        pltpu.VMEM((1, CH), F32),
        pltpu.VMEM((dp, 1, CH), F32),
        pltpu.VMEM((ROWS, width, CH), BF16),
        pltpu.VMEM((ROWS, width, CH), BF16),
        pltpu.SemaphoreType.DMA((12,)),
        pltpu.SemaphoreType.DMA((12, 3)),
        pltpu.SemaphoreType.DMA((8,)),
        pltpu.SemaphoreType.DMA((8,)),
        pltpu.SemaphoreType.DMA((2,)),
    ]
    results = pl.pallas_call(
        functools.partial(kernel, n, dp),
        out_shape=shapes,
        in_specs=[pl.BlockSpec(memory_space=pl.ANY)] * 7,
        out_specs=[pl.BlockSpec(memory_space=pl.ANY)] * 2 + [vmem] * 3,
        scratch_shapes=scratch,
        compiler_params=pltpu.CompilerParams(
            collective_id=0, has_side_effects=True, vmem_limit_bytes=62 * 1024 * 1024
        ),
    )(
        pair_in[0], residue_mask, chain_index, chain_bias.reshape(1, CH),
        proj_weight, out_weight, cotangent[0],
    )
    anywhere = pl.BlockSpec(memory_space=pl.ANY)
    out_pair, pair_grad, grad_proj, grad_out, grad_chain = pl.pallas_call(
        hand_over,
        out_shape=shapes,
        in_specs=[anywhere] * 5,
        out_specs=[anywhere] * 5,
        scratch_shapes=[pltpu.VMEM(shape.shape, shape.dtype) for shape in shapes]
        + [pltpu.SemaphoreType.DMA((13,)), pltpu.SemaphoreType.DMA((13,))],
        compiler_params=pltpu.CompilerParams(vmem_limit_bytes=62 * 1024 * 1024),
    )(*results)
    return out_pair[None], pair_grad[None], grad_proj, grad_out, grad_chain.reshape(CH)


def solution(mesh):
    n, dp = mesh.shape["dap"], mesh.shape["dp"]
    rows = P("dp", "dap", None, None)
    return jax.shard_map(
        functools.partial(body, n, dp),
        mesh=mesh,
        in_specs=(rows, P("dp", None), P("dp", None), P(), P(), P(), rows),
        out_specs=(rows, rows, P(), P(), P()),
        check_vma=False,
    )
```
